256 devices in a mesh: frames: 8 (over z), segments: 4 (over y), coils: 8 (over x, core).
Axes of the slice: x: 4, y: 4, z: 8, core: 2. Of those that a mesh axis runs over, the one named last changes fastest.
Arguments:
- x_in: float32 [8, 2, 2, 256, 256], P('frames', None, None, ('segments', 'coils')), may hold values from -6 to 6
- r_in: float32 [8, 2, 2, 256, 256], P('frames', None, None, ('segments', 'coils')), may hold values from -6 to 6
- p_in: float32 [8, 2, 2, 256, 256], P('frames', None, None, ('segments', 'coils')), may hold values from -6 to 6
- sens: bfloat16 [16, 2, 2, 256, 256], P('coils'), may hold values from -1 to 1
- seg_weights: bfloat16 [12, 8, 2, 16, 256], P('segments'), may hold values from 0.19921875 to 1
- seg_freq: float32 [12], replicated, may hold values from -3 to 3
- band_ids: int32 [12, 8], replicated, may hold values from 0 to 15, as said below
- seg_count: int32 [12], replicated, may hold values from 1 to 8, as said below
- k_bands: int32 [8, 16], P('frames'), may hold values from 0 to 31, as said below
Outputs:
- x_out: float32 [8, 2, 2, 256, 256], P('frames', None, None, ('segments', 'coils'))
- r_out: float32 [8, 2, 2, 256, 256], P('frames', None, None, ('segments', 'coils'))
- p_out: float32 [8, 2, 2, 256, 256], P('frames', None, None, ('segments', 'coils'))
The draws below stay inside these ranges and needn't reach their ends.
Inputs may be any that keep to these rules, and one draw needn't show every extreme that they name: `band_ids`: the 8 entries of one segment name distinct image bands. `seg_count`: some segment uses all 8 blocks. `k_bands`: the 16 entries of one frame name distinct k-space bands.
All inputs are finite; a program needn't handle non-finite values.
Results may differ from the reference program's by a relative error of at most 0.0028.
Values may be sent and summed in bfloat16 or wider, within the bound.
No kernel may reach another device: no remote copies, remote signals or barrier semaphores. Data moves between devices by JAX's collectives and lax.ppermute only.
A program may use at most 64 MiB of HBM per device.

```python
import math
import jax
import jax.numpy as jnp
from jax import lax

NX = 256
NY = 256
NCOIL = 16
NSEG = 12
PLANES = 2
BR = 16
OT = 8
KB = 8
KT = 16
NB = 16
NKB = 32
KR = 128
FRAMES = 8


def segment_lists(key):
    base = jax.random.fold_in(key, 7)
    keys = jax.random.split(base, NSEG + 2)
    band_lists = jax.vmap(lambda one_key: jax.random.permutation(one_key, NB)[:OT])(keys[:NSEG])
    counts = jax.random.randint(keys[NSEG], (NSEG,), 1, OT + 1)
    fullest = jax.random.randint(keys[NSEG + 1], (), 0, NSEG)
    counts = jnp.where(jnp.arange(NSEG, dtype=jnp.int32) == fullest, OT, counts)
    return (band_lists.astype(jnp.int32), counts.astype(jnp.int32))


def draw_band_ids(key, part):
    return segment_lists(key)[0]


def draw_seg_count(key, part):
    return segment_lists(key)[1]


def draw_k_bands(key, part):
    base = jax.random.fold_in(key, 11)
    keys = jax.random.split(base, FRAMES)
    return jax.vmap(lambda one_key: jax.random.permutation(one_key, NKB)[:KT])(keys).astype(jnp.int32)


def steps_of(own_key, extent, pieces, least, high):
    def one(axis_at, blocks):
        draws = jax.random.uniform(jax.random.fold_in(jax.random.fold_in(own_key, 6), axis_at), (blocks,), jnp.float32, least / len(pieces), high / len(pieces))
        return jnp.repeat(jnp.exp(draws), extent[axis_at] // blocks).reshape((-1,) + (1,) * (len(extent) - axis_at - 1))

    gain = one(*pieces[0])
    for cut in pieces[1:]:
        gain = gain * one(*cut)
    return gain


def scatter_about(rng, shape, scale, limit, shards=(), kind=jnp.bfloat16):
    values = scale * jax.random.normal(rng, shape, jnp.float32)
    if shards:
        values = values * steps_of(rng, shape, shards, -0.22, 0.18)
    return jnp.clip(values, -limit, limit).astype(kind)


def setup_inputs(seed: int = 0) -> dict:
    arg_keys = jax.random.split(jax.random.key(seed), 10)
    return {
        "x_in": scatter_about(arg_keys[0], (FRAMES, PLANES, 2, NY, NX), 1.0, 6.0, ((0, 8), (3, 32)), jnp.float32),
        "r_in": scatter_about(arg_keys[1], (FRAMES, PLANES, 2, NY, NX), 1.0, 6.0, ((0, 8), (3, 32)), jnp.float32),
        "p_in": scatter_about(arg_keys[2], (FRAMES, PLANES, 2, NY, NX), 1.0, 6.0, ((0, 8), (3, 32)), jnp.float32),
        "sens": scatter_about(arg_keys[3], (NCOIL, PLANES, 2, NY, NX), 0.18, 1.0, ((0, 8),)),
        "seg_weights": jnp.clip(0.19921875 + 0.80078125 * jax.random.uniform(arg_keys[4], (NSEG, OT, PLANES, BR, NX), jnp.float32) ** steps_of(arg_keys[4], (NSEG, OT, PLANES, BR, NX), ((0, 4),), -0.2, 0.2), 0.19921875, 1.0).astype(jnp.bfloat16),
        "seg_freq": jnp.clip(jax.random.uniform(arg_keys[5], (NSEG,), jnp.float32, -3.0, 3.0), -3.0, 3.0),
        "band_ids": draw_band_ids(jax.random.fold_in(arg_keys[9], 71), 0),
        "seg_count": draw_seg_count(jax.random.fold_in(arg_keys[9], 71), 0),
        "k_bands": draw_k_bands(jax.random.fold_in(arg_keys[9], 71), 0),
    }


reg_weight = 0.5
shift_weight = 0.1
epsilon = 1e-06

def widen(values):
    return values.astype(jnp.float32)

def contract(form, left, right):
    return jnp.einsum(form, widen(left), widen(right))

def fourier_parts(products, length):
    angle = (products % length).astype(jnp.float32) * (2.0 * math.pi / length)
    scale = 1.0 / math.sqrt(length)
    return ((jnp.cos(angle) * scale).astype(jnp.bfloat16), (-jnp.sin(angle) * scale).astype(jnp.bfloat16))

def readout_time(k_index, height, width):
    half_h = height // 2
    half_w = width // 2
    centred_k = ((k_index + half_h) % height - half_h).astype(jnp.float32) / half_h
    centred_x = ((jnp.arange(width, dtype=jnp.int32) + half_w) % width - half_w).astype(jnp.float32) / half_w
    return jnp.sqrt(centred_k[..., :, None] ** 2 + centred_x ** 2)

def frame_normal(p_frame, k_list, sens, seg_weights, seg_freq, band_ids, seg_count):
    k_index = (k_list[:, None] * KB + jnp.arange(KB, dtype=jnp.int32)[None, :]).reshape(KR)
    y_index = (band_ids[:, :, None] * BR + jnp.arange(BR, dtype=jnp.int32)[None, None, :]).reshape(NSEG, OT * BR)
    gy_re, gy_im = fourier_parts(k_index[None, :, None] * y_index[:, None, :], NY)
    columns = jnp.arange(NX, dtype=jnp.int32)
    gx_re, gx_im = fourier_parts(columns[:, None] * columns[None, :], NX)
    elapsed = readout_time(k_index, NY, NX)
    theta = seg_freq[:, None, None] * elapsed[None]
    cosine = jnp.cos(theta)
    sine = jnp.sin(theta)
    live = (jnp.arange(OT, dtype=jnp.int32)[None, :] < seg_count[:, None]).astype(jnp.float32)
    weights = widen(seg_weights) * live[:, :, None, None, None]
    weights = jnp.transpose(weights, (2, 0, 1, 3, 4))
    dir_re = p_frame[:, 0]
    dir_im = p_frame[:, 1]

    def one_coil(total, sens_coil):
        sens_re = widen(sens_coil[:, 0])
        sens_im = widen(sens_coil[:, 1])
        coil_re = sens_re * dir_re - sens_im * dir_im
        coil_im = sens_re * dir_im + sens_im * dir_re
        block_re = (coil_re.reshape(PLANES, NB, BR, NX)[:, band_ids] * weights).astype(jnp.bfloat16).reshape(PLANES, NSEG, OT * BR, NX)
        block_im = (coil_im.reshape(PLANES, NB, BR, NX)[:, band_ids] * weights).astype(jnp.bfloat16).reshape(PLANES, NSEG, OT * BR, NX)
        first_re = (contract('skm,qsmx->qskx', gy_re, block_re) - contract('skm,qsmx->qskx', gy_im, block_im)).astype(jnp.bfloat16)
        first_im = (contract('skm,qsmx->qskx', gy_re, block_im) + contract('skm,qsmx->qskx', gy_im, block_re)).astype(jnp.bfloat16)
        spec_re = contract('qskx,xz->qskz', first_re, gx_re) - contract('qskx,xz->qskz', first_im, gx_im)
        spec_im = contract('qskx,xz->qskz', first_re, gx_im) + contract('qskx,xz->qskz', first_im, gx_re)
        kspace_re = lax.optimization_barrier(jnp.sum(spec_re * cosine + spec_im * sine, axis=1))
        kspace_im = lax.optimization_barrier(jnp.sum(spec_im * cosine - spec_re * sine, axis=1))
        demod_re = (kspace_re[:, None] * cosine - kspace_im[:, None] * sine).astype(jnp.bfloat16)
        demod_im = (kspace_im[:, None] * cosine + kspace_re[:, None] * sine).astype(jnp.bfloat16)
        back_re = (contract('qskz,zx->qskx', demod_re, gx_re) + contract('qskz,zx->qskx', demod_im, gx_im)).astype(jnp.bfloat16)
        back_im = (contract('qskz,zx->qskx', demod_im, gx_re) - contract('qskz,zx->qskx', demod_re, gx_im)).astype(jnp.bfloat16)
        band_re = contract('skm,qskx->qsmx', gy_re, back_re) + contract('skm,qskx->qsmx', gy_im, back_im)
        band_im = contract('skm,qskx->qsmx', gy_re, back_im) - contract('skm,qskx->qsmx', gy_im, back_re)
        band_re = band_re.reshape(PLANES, NSEG, OT, BR, NX) * weights
        band_im = band_im.reshape(PLANES, NSEG, OT, BR, NX) * weights
        placed_re = jnp.zeros((PLANES, NB, BR, NX), jnp.float32).at[:, band_ids].add(band_re).reshape(PLANES, NY, NX)
        placed_im = jnp.zeros((PLANES, NB, BR, NX), jnp.float32).at[:, band_ids].add(band_im).reshape(PLANES, NY, NX)
        image_re = sens_re * placed_re + sens_im * placed_im
        image_im = sens_re * placed_im - sens_im * placed_re
        return (total + jnp.stack([image_re, image_im], axis=1), None)
    start = jnp.zeros((PLANES, 2, NY, NX), jnp.float32)
    total, _ = lax.scan(one_coil, start, sens)
    return total

def reference(x_in, r_in, p_in, sens, seg_weights, seg_freq, band_ids, seg_count, k_bands):
    normal = lax.map(lambda pair: frame_normal(pair[0], pair[1], sens, seg_weights, seg_freq, band_ids, seg_count), (p_in, k_bands))
    smooth = 2.0 * p_in - jnp.roll(p_in, 1, axis=0) - jnp.roll(p_in, -1, axis=0)
    applied = normal + reg_weight * smooth + shift_weight * p_in
    norm_now = jnp.sum(r_in * r_in)
    curvature = jnp.sum(p_in * applied)
    alpha = norm_now / (curvature + epsilon)
    x_out = x_in + alpha * p_in
    r_out = r_in - alpha * applied
    norm_next = jnp.sum(r_out * r_out)
    p_out = r_out + norm_next / (norm_now + epsilon) * p_in
    return (x_out, r_out, p_out)
```

```python
import math

import jax
import jax.numpy as jnp
from jax import lax
from jax.experimental import pallas as pl
from jax.experimental.pallas import tpu as pltpu
from jax.sharding import PartitionSpec as P

BR = 16
KB = 8
NX = 256
NY = 256
OT = 8
NSEG = 12
KR = 128
SEGS_DEV = 3
YDEV = 4
GROUP = 32
ROWS = 8

reg_weight = 0.5
shift_weight = 0.1
epsilon = 1e-06

F32 = jnp.float32
BF16 = jnp.bfloat16
SPACE = ("segments", "coils")


def sin_cos(angle):
    half = angle * 0.5
    sq = half * half
    s = F32(1.0 / math.factorial(13))
    for n in (11, 9, 7, 5, 3, 1):
        s = s * sq + F32((-1.0) ** (n // 2) / math.factorial(n))
    s = s * half
    c = F32(1.0 / math.factorial(16))
    for n in (14, 12, 10, 8, 6, 4, 2, 0):
        c = c * sq + F32((-1.0) ** (n // 2) / math.factorial(n))
    return 2.0 * s * c, 1.0 - 2.0 * s * s


def unit_parts(products):
    n = ((products + 128) & 255) - 128
    s, c = sin_cos(n.astype(F32) * F32(2.0 * math.pi / 256))
    return c * F32(1.0 / 16.0), s * F32(-1.0 / 16.0)


def segment_of(slot):
    y = lax.axis_index("segments")
    return lax.rem(y - slot // SEGS_DEV + YDEV, YDEV) * SEGS_DEV + slot % SEGS_DEV


def tables_kernel(bands_ref, kb_ref, freq_ref, g_ref, gt_ref, gx_ref, gxt_ref, cs_ref, sn_ref):
    def spread(values, index, width):
        out = jnp.zeros_like(index)
        for j, value in enumerate(values):
            out = jnp.where(index // width == j, value * width + index % width, out)
        return out

    kbs = [kb_ref[0, j] for j in range(KR // KB)]
    ky_col = spread(kbs, lax.broadcasted_iota(jnp.int32, (KR, KR), 0), KB)
    ky_row = spread(kbs, lax.broadcasted_iota(jnp.int32, (KR, KR), 1), KB)
    rows = lax.broadcasted_iota(jnp.int32, (NX, NX), 0)
    cols = lax.broadcasted_iota(jnp.int32, (NX, NX), 1)
    gre, gim = unit_parts(rows * cols)
    gre, gim, ngim = gre.astype(BF16), gim.astype(BF16), (-gim).astype(BF16)
    gx_ref[:NX, :NX] = gre
    gx_ref[:NX, NX:] = gim
    gx_ref[NX:, :NX] = ngim
    gx_ref[NX:, NX:] = gre
    gxt_ref[:NX, :NX] = gre
    gxt_ref[:NX, NX:] = ngim
    gxt_ref[NX:, :NX] = gim
    gxt_ref[NX:, NX:] = gre
    cy = (((ky_col + 128) & 255) - 128).astype(F32) * F32(1.0 / 128.0)
    cy = jnp.concatenate([cy, cy], axis=1)
    cx_index = lax.broadcasted_iota(jnp.int32, (KR, NX), 1)
    cx = (((cx_index + 128) & 255) - 128).astype(F32) * F32(1.0 / 128.0)
    elapsed = jnp.sqrt(cy * cy + cx * cx)

    @pl.loop(0, NSEG)
    def _(slot):
        seg = segment_of(slot)
        s, c = sin_cos(freq_ref[seg] * elapsed)
        cs_ref[slot] = c
        sn_ref[slot] = s
        bands = [bands_ref[seg, j] for j in range(OT)]
        yr_row = spread(bands, lax.broadcasted_iota(jnp.int32, (KR, KR), 1), BR)
        yr_col = spread(bands, lax.broadcasted_iota(jnp.int32, (KR, KR), 0), BR)
        re, im = unit_parts(ky_col * yr_row)
        g_ref[slot, :KR, :KR] = re.astype(BF16)
        g_ref[slot, :KR, KR:] = (-im).astype(BF16)
        g_ref[slot, KR:, :KR] = im.astype(BF16)
        g_ref[slot, KR:, KR:] = re.astype(BF16)
        re, im = unit_parts(yr_col * ky_row)
        gt_ref[slot, :KR, :KR] = re.astype(BF16)
        gt_ref[slot, :KR, KR:] = im.astype(BF16)
        gt_ref[slot, KR:, :KR] = (-im).astype(BF16)
        gt_ref[slot, KR:, KR:] = re.astype(BF16)


def mm(a, b):
    return jnp.dot(a, b, preferred_element_type=F32)


def normal_kernel(
    bands_ref, count_ref, p_ref, sens_ref, w0_ref, w1_ref, w2_ref, w3_ref,
    g_ref, gt_ref, gx_ref, gxt_ref, cs_ref, sn_ref, out_ref,
    coil, blk, first, ks, acc,
):
    w_refs = (w0_ref, w1_ref, w2_ref, w3_ref)
    sre = sens_ref[0].astype(F32)
    sim = sens_ref[1].astype(F32)
    pre = p_ref[:, 0].reshape(NY, NX)
    pim = p_ref[:, 1].reshape(NY, NX)
    coil[0] = sre * pre - sim * pim
    coil[1] = sre * pim + sim * pre
    acc[...] = jnp.zeros_like(acc)
    for slot in range(NSEG):
        seg = segment_of(slot)
        count = count_ref[seg]
        for j in range(OT):
            live = (j < count).astype(F32)
            at = pl.ds(pl.multiple_of(bands_ref[seg, j] * BR, BR), BR)
            w = w_refs[slot // SEGS_DEV][slot % SEGS_DEV, j].astype(F32) * live
            blk[slot % 2, j * BR : (j + 1) * BR] = (coil[0, at] * w).astype(BF16)
            blk[slot % 2, KR + j * BR : KR + (j + 1) * BR] = (coil[1, at] * w).astype(BF16)
        got = mm(g_ref[slot], blk[slot % 2]).astype(BF16)
        first[slot * KR : (slot + 1) * KR, :NX] = got[:KR]
        first[slot * KR : (slot + 1) * KR, NX:] = got[KR:]
    for slot in range(NSEG):
        spec = mm(first[slot * KR : (slot + 1) * KR], gx_ref[...])
        re, im = spec[:, :NX], spec[:, NX:]
        c, s = cs_ref[slot], sn_ref[slot]
        if slot == 0:
            ks[:, :NX] = re * c + im * s
            ks[:, NX:] = im * c - re * s
        else:
            ks[:, :NX] += re * c + im * s
            ks[:, NX:] += im * c - re * s
    for slot in range(NSEG):
        seg = segment_of(slot)
        count = count_ref[seg]
        re, im = ks[:, :NX], ks[:, NX:]
        c, s = cs_ref[slot], sn_ref[slot]
        demod = jnp.concatenate([(re * c - im * s).astype(BF16), (im * c + re * s).astype(BF16)], axis=1)
        back = mm(demod, gxt_ref[...]).astype(BF16)
        band = mm(gt_ref[slot], jnp.concatenate([back[:, :NX], back[:, NX:]], axis=0))
        for j in range(OT):
            live = (j < count).astype(F32)
            at = pl.ds(pl.multiple_of(bands_ref[seg, j] * BR, BR), BR)
            w = w_refs[slot // SEGS_DEV][slot % SEGS_DEV, j].astype(F32) * live
            acc[0, at] += band[j * BR : (j + 1) * BR] * w
            acc[1, at] += band[KR + j * BR : KR + (j + 1) * BR] * w
    sre = sens_ref[0].astype(F32)
    sim = sens_ref[1].astype(F32)
    out_ref[:, 0] = (sre * acc[0] + sim * acc[1]).reshape(GROUP, ROWS, NX)
    out_ref[:, 1] = (sre * acc[1] - sim * acc[0]).reshape(GROUP, ROWS, NX)


def applied_kernel(parts_ref, r_ref, p_ref, low_ref, high_ref, applied_ref, sums_ref):
    totals = [jnp.zeros((ROWS, NX), F32) for _ in range(4)]
    for q in range(2):
        for c in range(2):
            total = jnp.zeros((ROWS, NX), F32)
            for half in range(2):
                for xc in range(8):
                    total = total + parts_ref[(half * 2 + q) * 8 + xc, c]
            p = p_ref[0, q, c]
            r = r_ref[0, q, c]
            smooth = 2.0 * p - low_ref[0, q, c].astype(F32) - high_ref[0, q, c].astype(F32)
            applied = total + reg_weight * smooth + shift_weight * p
            applied_ref[0, q, c] = applied
            for i, term in enumerate((r * r, p * applied, r * applied, applied * applied)):
                totals[i] = totals[i] + term
    sums_ref[...] = jnp.zeros_like(sums_ref)
    for i in range(4):
        line = jnp.sum(totals[i], axis=0, keepdims=True)
        sums_ref[i : i + 1] = line[:, :128] + line[:, 128:]


def update_kernel(sums_ref, x_ref, r_ref, p_ref, applied_ref, x_out, r_out, p_out):
    sums = jnp.sum(sums_ref[...], axis=1, keepdims=True)
    rr, pa, ra, aa = (sums[i : i + 1] for i in range(4))
    alpha = rr / (pa + epsilon)
    rnew = rr - 2.0 * alpha * ra + alpha * alpha * aa
    beta = rnew / (rr + epsilon)
    alpha = jnp.broadcast_to(alpha, (ROWS, NX))
    beta = jnp.broadcast_to(beta, (ROWS, NX))
    for q in range(2):
        for c in range(2):
            p = p_ref[0, q, c]
            r = r_ref[0, q, c] - alpha * applied_ref[0, q, c]
            x_out[0, q, c] = x_ref[0, q, c] + alpha * p
            r_out[0, q, c] = r
            p_out[0, q, c] = r + beta * p


VM = pl.BlockSpec(memory_space=pltpu.VMEM)
SM = pl.BlockSpec(memory_space=pltpu.SMEM)


def sum_all(v):
    def step(v, axes, perms):
        parts = [lax.ppermute(v, axes, perm) for perm in perms]
        return v + parts[0] + parts[1] + parts[2]

    v = step(v, "segments", [[(i, (i + k) % 4) for i in range(4)] for k in (1, 2, 3)])
    v = step(v, "coils", [[(i, (i + k) % 8) for i in range(8)] for k in (2, 4, 6)])
    v = step(v, "frames", [[(i, (i + k) % 8) for i in range(8)] for k in (2, 4, 6)])
    return step(v, ("frames", "coils"), [[(i, i ^ k) for i in range(64)] for k in (1, 8, 9)])


def local(x_in, r_in, p_in, sens, seg_weights, seg_freq, band_ids, seg_count, k_bands):
    y = lax.axis_index("segments")
    plane = lax.rem(y, 2)
    w_own = lax.dynamic_index_in_dim(seg_weights, plane, 2, keepdims=False)
    w_other = lax.dynamic_index_in_dim(seg_weights, 1 - plane, 2, keepdims=False)
    w_parts = [w_own] + [
        lax.ppermute(w_own if k == 2 else w_other, "segments", [(i, (i + k) % 4) for i in range(4)])
        for k in (1, 2, 3)
    ]
    halo = p_in.astype(BF16)
    low = lax.ppermute(halo, "frames", [(i, (i + 1) % 8) for i in range(8)])
    high = lax.ppermute(halo, "frames", [(i, (i + 7) % 8) for i in range(8)])
    send = jnp.broadcast_to(p_in[0][None, :, None], (2, 2, 8, 2, ROWS, NX)).reshape(GROUP, 2, ROWS, NX)
    whole = lax.all_to_all(send, SPACE, 0, 0, tiled=True)
    tables = pl.pallas_call(
        tables_kernel,
        in_specs=[SM, SM, SM],
        out_specs=[VM] * 6,
        out_shape=[
            jax.ShapeDtypeStruct((NSEG, 2 * KR, 2 * KR), BF16),
            jax.ShapeDtypeStruct((NSEG, 2 * KR, 2 * KR), BF16),
            jax.ShapeDtypeStruct((2 * NX, 2 * NX), BF16),
            jax.ShapeDtypeStruct((2 * NX, 2 * NX), BF16),
            jax.ShapeDtypeStruct((NSEG, KR, NX), F32),
            jax.ShapeDtypeStruct((NSEG, KR, NX), F32),
        ],
        compiler_params=pltpu.CompilerParams(vmem_limit_bytes=24 << 20),
        cost_estimate=pl.CostEstimate(flops=30_000_000, bytes_accessed=8 << 20, transcendentals=0),
        name="tables",
    )(band_ids, k_bands, seg_freq)
    sens_mine = lax.dynamic_slice(sens, (y // 2, plane, 0, 0, 0), (1, 1, 2, NY, NX)).reshape(2, NY, NX)
    parts = pl.pallas_call(
        normal_kernel,
        in_specs=[SM, SM] + [VM] * 12,
        out_specs=VM,
        out_shape=jax.ShapeDtypeStruct((GROUP, 2, ROWS, NX), F32),
        scratch_shapes=[
            pltpu.VMEM((2, NY, NX), F32),
            pltpu.VMEM((2, 2 * KR, NX), BF16),
            pltpu.VMEM((NSEG * KR, 2 * NX), BF16),
            pltpu.VMEM((KR, 2 * NX), F32),
            pltpu.VMEM((2, NY, NX), F32),
        ],
        compiler_params=pltpu.CompilerParams(vmem_limit_bytes=40 << 20),
        cost_estimate=pl.CostEstimate(flops=2_400_000_000, bytes_accessed=8 << 20, transcendentals=0),
        name="normal",
    )(band_ids, seg_count, whole, sens_mine, *w_parts, *tables)
    parts = lax.all_to_all(parts, SPACE, 0, 0, tiled=True)
    share = jax.ShapeDtypeStruct(p_in.shape, F32)
    applied, sums = pl.pallas_call(
        applied_kernel,
        in_specs=[VM] * 5,
        out_specs=[VM, VM],
        out_shape=[share, jax.ShapeDtypeStruct((8, 128), F32)],
        name="applied",
    )(parts, r_in, p_in, low, high)
    sums = sum_all(sums)
    return tuple(
        pl.pallas_call(
            update_kernel,
            in_specs=[VM] * 5,
            out_specs=[VM] * 3,
            out_shape=[share] * 3,
            name="update",
        )(sums, x_in, r_in, p_in, applied)
    )


def solution(mesh):
    image = P("frames", None, None, ("segments", "coils"), None)
    in_specs = (
        image,
        image,
        image,
        P("coils", None, None, None, None),
        P("segments", None, None, None, None),
        P(),
        P(),
        P(),
        P("frames", None),
    )
    return jax.shard_map(local, mesh=mesh, in_specs=in_specs, out_specs=(image,) * 3, check_vma=False)
```

```python
import math

import jax
import jax.numpy as jnp
from jax import lax
from jax.experimental import pallas as pl
from jax.experimental.pallas import tpu as pltpu
from jax.sharding import PartitionSpec as P

BR = 16
KB = 8
NX = 256
NY = 256
OT = 8
NSEG = 12
KR = 128
SEGS_DEV = 3
YDEV = 4
GROUP = 32
ROWS = 8
HALF = OT // 2
DEVICES = 256
CODE = 32767.0 / 6.0

reg_weight = 0.5
shift_weight = 0.1
epsilon = 1e-06

F32 = jnp.float32
BF16 = jnp.bfloat16
SPACE = ("segments", "coils")


def sin_cos(angle):
    half = angle * 0.5
    sq = half * half
    s = F32(1.0 / math.factorial(13))
    for n in (11, 9, 7, 5, 3, 1):
        s = s * sq + F32((-1.0) ** (n // 2) / math.factorial(n))
    s = s * half
    c = F32(1.0 / math.factorial(16))
    for n in (14, 12, 10, 8, 6, 4, 2, 0):
        c = c * sq + F32((-1.0) ** (n // 2) / math.factorial(n))
    return 2.0 * s * c, 1.0 - 2.0 * s * s


def unit_parts(products):
    n = ((products + 128) & 255) - 128
    s, c = sin_cos(n.astype(F32) * F32(2.0 * math.pi / 256))
    return c * F32(1.0 / 16.0), s * F32(-1.0 / 16.0)


def segment_of(slot):
    y = lax.axis_index("segments")
    return lax.rem(y - slot // SEGS_DEV + YDEV, YDEV) * SEGS_DEV + slot % SEGS_DEV


def block_of(place):
    core = lax.rem(lax.axis_index("coils"), 2)
    return lax.rem(core * HALF + place, OT)


def prep_kernel(p_ref, w_ref, send_ref, same_ref, other_ref, sem):
    plane = lax.rem(lax.axis_index("segments"), 2)
    first_block = lax.rem(lax.axis_index("coils"), 2) * HALF
    blocks = pl.ds(first_block, HALF)
    copies = [
        pltpu.make_async_copy(w_ref.at[:, blocks, plane], same_ref, sem.at[0]),
        pltpu.make_async_copy(w_ref.at[:, blocks, 1 - plane], other_ref, sem.at[1]),
    ]
    for copy in copies:
        copy.start()
    for q in range(2):
        both = jnp.concatenate([p_ref[0, q, 0], p_ref[0, q, 1]], axis=0)
        code = jnp.floor(both * F32(CODE) + 0.5).astype(jnp.int32).astype(jnp.int16)
        for pair in range(2):
            for xc in range(8):
                send_ref[(pair * 2 + q) * 8 + xc] = code
    for copy in copies:
        copy.wait()


def tables_kernel(
    bands_ref, kb_ref, freq_ref, sens_ref, w_ref,
    g_out, mine_out, own_out, gt_out, gx_out, turn_out,
    g, gt, gx, turn, ft, e, g_sem, gt_sem, turn_sem, sem,
):
    y = lax.axis_index("segments")
    plane = lax.rem(y, 2)
    copies = [
        pltpu.make_async_copy(sens_ref.at[y // 2, plane], mine_out, sem.at[0]),
        pltpu.make_async_copy(w_ref.at[:, :, plane], own_out, sem.at[1]),
        pltpu.make_async_copy(gx, gx_out, sem.at[2]),
    ]
    copies[0].start()
    copies[1].start()

    def spread(values, index, width):
        out = jnp.zeros_like(index)
        for j, value in enumerate(values):
            out = jnp.where(index // width == j, value * width + index % width, out)
        return out

    kbs = [kb_ref[0, j] for j in range(KR // KB)]
    ky_col = spread(kbs, lax.broadcasted_iota(jnp.int32, (KR, KR), 0), KB)
    ky_row = spread(kbs, lax.broadcasted_iota(jnp.int32, (8, KR), 1), KB)[:1]
    rows = lax.broadcasted_iota(jnp.int32, (NX, NX), 0)
    cols = lax.broadcasted_iota(jnp.int32, (NX, NX), 1)
    gre, gim = unit_parts(rows * cols)
    gre, gim, ngim = gre.astype(BF16), gim.astype(BF16), (-gim).astype(BF16)
    gx[0, :NX, :NX] = gre
    gx[0, :NX, NX:] = gim
    gx[0, NX:, :NX] = ngim
    gx[0, NX:, NX:] = gre
    gx[1, :NX, :NX] = gre
    gx[1, :NX, NX:] = ngim
    gx[1, NX:, :NX] = gim
    gx[1, NX:, NX:] = gre
    copies[2].start()
    re, im = unit_parts(lax.broadcasted_iota(jnp.int32, (NY, KR), 0) * ky_row)
    ft[0, :, :KR] = re.astype(BF16)
    ft[0, :, KR:] = im.astype(BF16)
    ft[1, :, :KR] = (-im).astype(BF16)
    ft[1, :, KR:] = re.astype(BF16)
    ky_wide = jnp.concatenate([ky_col, ky_col], axis=1)
    re, im = unit_parts(ky_wide * lax.broadcasted_iota(jnp.int32, (KR, NY), 1))
    e[0, :KR] = re.astype(BF16)
    e[0, KR:] = im.astype(BF16)
    e[1, :KR] = (-im).astype(BF16)
    e[1, KR:] = re.astype(BF16)
    cy = (((ky_wide + 128) & 255) - 128).astype(F32) * F32(1.0 / 128.0)
    cx_index = lax.broadcasted_iota(jnp.int32, (KR, NX), 1)
    cx = (((cx_index + 128) & 255) - 128).astype(F32) * F32(1.0 / 128.0)
    elapsed = jnp.sqrt(cy * cy + cx * cx)
    image_row = lax.broadcasted_iota(jnp.int32, (NY, KR), 0)

    def saves(slot):
        return (
            pltpu.make_async_copy(g.at[slot], g_out.at[slot], g_sem.at[slot]),
            pltpu.make_async_copy(gt.at[slot], gt_out.at[slot], gt_sem.at[slot]),
            pltpu.make_async_copy(turn.at[slot], turn_out.at[slot], turn_sem.at[slot]),
        )

    @pl.loop(0, NSEG)
    def _(slot):
        seg = segment_of(slot)
        s, c = sin_cos(freq_ref[seg] * elapsed)
        turn[slot, 0] = c
        turn[slot, 1] = s
        bands = [bands_ref[seg, block_of(t)] for t in range(OT)]
        yr_row = spread(bands, lax.broadcasted_iota(jnp.int32, (8, KR), 1), BR)[:1]
        pick = jnp.where(image_row == yr_row, F32(1), F32(0)).astype(BF16)
        g[slot, :, :KR] = mm(e[0], pick).astype(BF16)
        g[slot, :, KR:] = mm(e[1], pick).astype(BF16)
        for t in range(OT):
            at = pl.ds(pl.multiple_of(bands[t] * BR, BR), BR)
            gt[slot, t * BR : (t + 1) * BR] = ft[0, at]
            gt[slot, KR + t * BR : KR + (t + 1) * BR] = ft[1, at]
        for copy in saves(slot):
            copy.start()

    @pl.loop(0, NSEG)
    def _(slot):
        for copy in saves(slot):
            copy.wait()

    for copy in copies:
        copy.wait()


def mm(a, b):
    return jnp.dot(a, b, preferred_element_type=F32)


def normal_kernel(
    bands_ref, count_ref, p_ref, mine_in, own_in, g_in, h1_in, o1_in, h2_in, o2_in, h3_in, o3_in,
    gx_in, turn_in, gt_in, out_ref,
    coil, blk, first, ks, acc, mine, own, far, g, gx, turn, gt, sem,
):
    pieces = [(mine_in, mine), (own_in, own), (g_in.at[:SEGS_DEV], g.at[:SEGS_DEV])]
    pieces += [(g_in.at[SEGS_DEV:], g.at[SEGS_DEV:])]
    pieces += [(half, far.at[i]) for i, half in enumerate((h1_in, o1_in, h2_in, o2_in, h3_in, o3_in))]
    pieces += [(gx_in, gx), (turn_in, turn), (gt_in, gt)]
    loads = [pltpu.make_async_copy(source, target, sem.at[i]) for i, (source, target) in enumerate(pieces)]
    for load in loads:
        load.start()
    loads[0].wait()

    def weight(slot, t, seg):
        k, i = slot // SEGS_DEV, slot % SEGS_DEV
        j = block_of(t)
        live = (j < count_ref[seg]).astype(F32)
        if k == 0:
            w = own[i, j]
        else:
            w = far[2 * (k - 1) + t // HALF, i, t % HALF]
        at = pl.ds(pl.multiple_of(bands_ref[seg, j] * BR, BR), BR)
        return w.astype(F32) * live, at

    sre = mine[0].astype(F32)
    sim = mine[1].astype(F32)
    p = p_ref[...].astype(jnp.int32).astype(F32) * F32(1.0 / CODE)
    pre = p[:, :ROWS].reshape(NY, NX)
    pim = p[:, ROWS:].reshape(NY, NX)
    coil[0] = sre * pre - sim * pim
    coil[1] = sre * pim + sim * pre
    acc[...] = jnp.zeros_like(acc)
    for slot in range(NSEG):
        seg = segment_of(slot)
        if slot == 0:
            loads[1].wait()
            loads[2].wait()
        elif slot % SEGS_DEV == 0:
            k = slot // SEGS_DEV
            if k == 1:
                loads[3].wait()
            loads[2 * k + 2].wait()
            loads[2 * k + 3].wait()
        for t in range(OT):
            w, at = weight(slot, t, seg)
            blk[slot % 2, t * BR : (t + 1) * BR] = (coil[0, at] * w).astype(BF16)
            blk[slot % 2, KR + t * BR : KR + (t + 1) * BR] = (coil[1, at] * w).astype(BF16)
        got = mm(g[slot], blk[slot % 2]).astype(BF16)
        first[slot * KR : (slot + 1) * KR, :NX] = got[:KR]
        first[slot * KR : (slot + 1) * KR, NX:] = got[KR:]
    loads[10].wait()
    loads[11].wait()
    for pair in range(NSEG // 2):
        spec = mm(first[pair * 2 * KR : (pair + 1) * 2 * KR], gx[0])
        tre, tim = 0.0, 0.0
        for half in range(2):
            re, im = spec[half * KR : (half + 1) * KR, :NX], spec[half * KR : (half + 1) * KR, NX:]
            c, s = turn[pair * 2 + half, 0], turn[pair * 2 + half, 1]
            tre = tre + (re * c + im * s)
            tim = tim + (im * c - re * s)
        if pair == 0:
            ks[:, :NX] = tre
            ks[:, NX:] = tim
        else:
            ks[:, :NX] += tre
            ks[:, NX:] += tim
    loads[12].wait()
    for pair in range(NSEG // 2):
        for half in range(2):
            re, im = ks[:, :NX], ks[:, NX:]
            c, s = turn[pair * 2 + half, 0], turn[pair * 2 + half, 1]
            here = slice((pair * 2 + half) * KR, (pair * 2 + half + 1) * KR)
            first[here, :NX] = (re * c - im * s).astype(BF16)
            first[here, NX:] = (im * c + re * s).astype(BF16)
        back = mm(first[pair * 2 * KR : (pair + 1) * 2 * KR], gx[1]).astype(BF16)
        for half in range(2):
            slot = pair * 2 + half
            seg = segment_of(slot)
            mid = back[half * KR : (half + 1) * KR]
            band = mm(gt[slot], jnp.concatenate([mid[:, :NX], mid[:, NX:]], axis=0))
            for t in range(OT):
                w, at = weight(slot, t, seg)
                acc[0, at] += band[t * BR : (t + 1) * BR] * w
                acc[1, at] += band[KR + t * BR : KR + (t + 1) * BR] * w
    sre = mine[0].astype(F32)
    sim = mine[1].astype(F32)
    out_re = (sre * acc[0] + sim * acc[1]).reshape(GROUP, ROWS, NX)
    out_im = (sre * acc[1] - sim * acc[0]).reshape(GROUP, ROWS, NX)
    out_ref[...] = jnp.concatenate([out_re, out_im], axis=1).astype(BF16)


def applied_kernel(parts_ref, r_ref, p_ref, low_ref, high_ref, applied_ref, sums_ref):
    totals = [jnp.zeros((ROWS, NX), F32) for _ in range(4)]
    for q in range(2):
        total = jnp.zeros((2 * ROWS, NX), F32)
        for pair in range(2):
            for xc in range(8):
                total = total + parts_ref[(pair * 2 + q) * 8 + xc].astype(F32)
        for c in range(2):
            p = p_ref[0, q, c]
            r = r_ref[0, q, c]
            smooth = 2.0 * p - low_ref[0, q, c].astype(F32) - high_ref[0, q, c].astype(F32)
            applied = total[c * ROWS : (c + 1) * ROWS] + reg_weight * smooth + shift_weight * p
            applied_ref[0, q, c] = applied
            for i, term in enumerate((r * r, p * applied, r * applied, applied * applied)):
                totals[i] = totals[i] + term
    lane = lax.broadcasted_iota(jnp.int32, (8, 128), 1)
    line = jnp.zeros((8, 128), F32)
    for i in range(4):
        whole = jnp.sum(jnp.sum(totals[i], axis=0, keepdims=True), axis=1, keepdims=True)
        line = jnp.where(lane == i, whole, line)
    sums_ref[...] = jnp.broadcast_to(line[:1, :8], (DEVICES, 8))


def update_kernel(sums_ref, x_ref, r_ref, p_ref, applied_ref, x_out, r_out, p_out):
    sums = jnp.sum(sums_ref[...], axis=0, keepdims=True)
    rr, pa, ra, aa = (sums[:, i : i + 1] for i in range(4))
    alpha = rr / (pa + epsilon)
    rnew = rr - 2.0 * alpha * ra + alpha * alpha * aa
    beta = rnew / (rr + epsilon)
    alpha = jnp.broadcast_to(alpha, (ROWS, NX))
    beta = jnp.broadcast_to(beta, (ROWS, NX))
    for q in range(2):
        for c in range(2):
            p = p_ref[0, q, c]
            r = r_ref[0, q, c] - alpha * applied_ref[0, q, c]
            x_out[0, q, c] = x_ref[0, q, c] + alpha * p
            r_out[0, q, c] = r
            p_out[0, q, c] = r + beta * p


VM = pl.BlockSpec(memory_space=pltpu.VMEM)
SM = pl.BlockSpec(memory_space=pltpu.SMEM)
HB = pl.BlockSpec(memory_space=pltpu.HBM)


def hbm(array):
    return pltpu.with_memory_space_constraint(array, pltpu.HBM)


def local(x_in, r_in, p_in, sens, seg_weights, seg_freq, band_ids, seg_count, k_bands):
    send, same, other = pl.pallas_call(
        prep_kernel,
        in_specs=[VM, HB],
        out_specs=[VM, HB, HB],
        out_shape=[jax.ShapeDtypeStruct((GROUP, 2 * ROWS, NX), jnp.int16)] + [pltpu.HBM((SEGS_DEV, HALF, BR, NX), BF16)] * 2,
        scratch_shapes=[pltpu.SemaphoreType.DMA((2,))],
        compiler_params=pltpu.CompilerParams(vmem_limit_bytes=4 << 20),
        name="prep",
    )(p_in, hbm(seg_weights))
    halves = [
        lax.ppermute(same if k == 2 else other, "segments", [(i, (i + k) % 4) for i in range(4)])
        for k in (1, 2, 3)
    ]
    others = [lax.ppermute(half, "coils", [(i, i ^ 1) for i in range(8)]) for half in halves]
    whole = lax.all_to_all(send, SPACE, 0, 0, tiled=True)
    halo = p_in.astype(BF16)
    low = lax.ppermute(halo, "frames", [(i, (i + 1) % 8) for i in range(8)])
    high = lax.ppermute(halo, "frames", [(i, (i + 7) % 8) for i in range(8)])
    g, mine, own, gt, gx, turn = pl.pallas_call(
        tables_kernel,
        in_specs=[SM, SM, SM, HB, HB],
        out_specs=[HB] * 6,
        out_shape=[
            pltpu.HBM((NSEG, 2 * KR, 2 * KR), BF16),
            pltpu.HBM((2, NY, NX), BF16),
            pltpu.HBM((SEGS_DEV, OT, BR, NX), BF16),
            pltpu.HBM((NSEG, 2 * KR, 2 * KR), BF16),
            pltpu.HBM((2, 2 * NX, 2 * NX), BF16),
            pltpu.HBM((NSEG, 2, KR, NX), F32),
        ],
        scratch_shapes=[
            pltpu.VMEM((NSEG, 2 * KR, 2 * KR), BF16),
            pltpu.VMEM((NSEG, 2 * KR, 2 * KR), BF16),
            pltpu.VMEM((2, 2 * NX, 2 * NX), BF16),
            pltpu.VMEM((NSEG, 2, KR, NX), F32),
            pltpu.VMEM((2, NY, 2 * KR), BF16),
            pltpu.VMEM((2, 2 * KR, NY), BF16),
            pltpu.SemaphoreType.DMA((NSEG,)),
            pltpu.SemaphoreType.DMA((NSEG,)),
            pltpu.SemaphoreType.DMA((NSEG,)),
            pltpu.SemaphoreType.DMA((3,)),
        ],
        compiler_params=pltpu.CompilerParams(vmem_limit_bytes=32 << 20),
        cost_estimate=pl.CostEstimate(flops=30_000_000, bytes_accessed=8 << 20, transcendentals=0),
        name="tables",
    )(band_ids, k_bands, seg_freq, hbm(sens), hbm(seg_weights))
    parts = pl.pallas_call(
        normal_kernel,
        in_specs=[SM, SM, VM] + [HB] * 12,
        out_specs=VM,
        out_shape=jax.ShapeDtypeStruct((GROUP, 2 * ROWS, NX), BF16),
        scratch_shapes=[
            pltpu.VMEM((2, NY, NX), F32),
            pltpu.VMEM((2, 2 * KR, NX), BF16),
            pltpu.VMEM((NSEG * KR, 2 * NX), BF16),
            pltpu.VMEM((KR, 2 * NX), F32),
            pltpu.VMEM((2, NY, NX), F32),
            pltpu.VMEM((2, NY, NX), BF16),
            pltpu.VMEM((SEGS_DEV, OT, BR, NX), BF16),
            pltpu.VMEM((6, SEGS_DEV, HALF, BR, NX), BF16),
            pltpu.VMEM((NSEG, 2 * KR, 2 * KR), BF16),
            pltpu.VMEM((2, 2 * NX, 2 * NX), BF16),
            pltpu.VMEM((NSEG, 2, KR, NX), F32),
            pltpu.VMEM((NSEG, 2 * KR, 2 * KR), BF16),
            pltpu.SemaphoreType.DMA((13,)),
        ],
        compiler_params=pltpu.CompilerParams(vmem_limit_bytes=32 << 20),
        cost_estimate=pl.CostEstimate(flops=2_400_000_000, bytes_accessed=8 << 20, transcendentals=0),
        name="normal",
    )(
        band_ids, seg_count, whole, hbm(mine), hbm(own), hbm(g),
        *map(hbm, (halves[0], others[0], halves[1], others[1], halves[2], others[2])), hbm(gx), hbm(turn), hbm(gt),
    )
    parts = lax.all_to_all(parts, SPACE, 0, 0, tiled=True)
    share = jax.ShapeDtypeStruct(p_in.shape, F32)
    applied, sums = pl.pallas_call(
        applied_kernel,
        in_specs=[VM] * 5,
        out_specs=[VM, VM],
        out_shape=[share, jax.ShapeDtypeStruct((DEVICES, 8), F32)],
        compiler_params=pltpu.CompilerParams(vmem_limit_bytes=4 << 20),
        name="applied",
    )(parts, r_in, p_in, low, high)
    sums = lax.all_to_all(sums, ("frames", "segments", "coils"), 0, 0, tiled=True)
    return tuple(
        pl.pallas_call(
            update_kernel,
            in_specs=[VM] * 5,
            out_specs=[VM] * 3,
            out_shape=[share] * 3,
            compiler_params=pltpu.CompilerParams(vmem_limit_bytes=4 << 20),
            name="update",
        )(sums, x_in, r_in, p_in, applied)
    )


def solution(mesh):
    image = P("frames", None, None, ("segments", "coils"), None)
    in_specs = (
        image,
        image,
        image,
        P("coils", None, None, None, None),
        P("segments", None, None, None, None),
        P(),
        P(),
        P(),
        P("frames", None),
    )
    return jax.shard_map(local, mesh=mesh, in_specs=in_specs, out_specs=(image,) * 3, check_vma=False)
```

```python
import math

import jax
import jax.numpy as jnp
from jax import lax
from jax.experimental import pallas as pl
from jax.experimental.pallas import tpu as pltpu
from jax.sharding import PartitionSpec as P

BR = 16
KB = 8
NX = 256
NY = 256
OT = 8
NSEG = 12
KR = 128
SEGS_DEV = 3
YDEV = 4
GROUP = 32
ROWS = 8
HALF = OT // 2
DEVICES = 256
CODE = 32767.0 / 6.0

reg_weight = 0.5
shift_weight = 0.1
epsilon = 1e-06

F32 = jnp.float32
BF16 = jnp.bfloat16
SPACE = ("segments", "coils")


def sin_cos(angle):
    half = angle * 0.5
    sq = half * half
    s = F32(1.0 / math.factorial(13))
    for n in (11, 9, 7, 5, 3, 1):
        s = s * sq + F32((-1.0) ** (n // 2) / math.factorial(n))
    s = s * half
    c = F32(1.0 / math.factorial(16))
    for n in (14, 12, 10, 8, 6, 4, 2, 0):
        c = c * sq + F32((-1.0) ** (n // 2) / math.factorial(n))
    return 2.0 * s * c, 1.0 - 2.0 * s * s


def unit_parts(products):
    n = ((products + 128) & 255) - 128
    s, c = sin_cos(n.astype(F32) * F32(2.0 * math.pi / 256))
    return c * F32(1.0 / 16.0), s * F32(-1.0 / 16.0)


def segment_of(slot):
    y = lax.axis_index("segments")
    return lax.rem(y - slot // SEGS_DEV + YDEV, YDEV) * SEGS_DEV + slot % SEGS_DEV


def block_of(place):
    core = lax.rem(lax.axis_index("coils"), 2)
    return lax.rem(core * HALF + place, OT)


def prep_kernel(p_ref, w_ref, send_ref, same_ref, other_ref):
    plane = lax.rem(lax.axis_index("segments"), 2)
    core = lax.rem(lax.axis_index("coils"), 2)
    for i in range(SEGS_DEV):
        for t in range(HALF):
            same_ref[i, t] = w_ref[i, core * HALF + t, plane]
            other_ref[i, t] = w_ref[i, core * HALF + t, 1 - plane]
    for q in range(2):
        both = jnp.concatenate([p_ref[0, q, 0], p_ref[0, q, 1]], axis=0)
        code = jnp.floor(both * F32(CODE) + 0.5).astype(jnp.int32).astype(jnp.int16)
        for pair in range(2):
            for xc in range(8):
                send_ref[(pair * 2 + q) * 8 + xc] = code


def tables_kernel(
    bands_ref, kb_ref, freq_ref, g_out, gt_out, gx_out, turn_out,
    g, gt, gx, turn, ft, e, g_sem, gt_sem, turn_sem, sem,
):
    save_gx = pltpu.make_async_copy(gx, gx_out, sem.at[0])

    def spread(values, index, width):
        out = jnp.zeros_like(index)
        for j, value in enumerate(values):
            out = jnp.where(index // width == j, value * width + index % width, out)
        return out

    kbs = [kb_ref[0, j] for j in range(KR // KB)]
    ky_col = spread(kbs, lax.broadcasted_iota(jnp.int32, (KR, KR), 0), KB)
    ky_row = spread(kbs, lax.broadcasted_iota(jnp.int32, (8, KR), 1), KB)[:1]
    rows = lax.broadcasted_iota(jnp.int32, (NX, NX), 0)
    cols = lax.broadcasted_iota(jnp.int32, (NX, NX), 1)
    gre, gim = unit_parts(rows * cols)
    gre, gim, ngim = gre.astype(BF16), gim.astype(BF16), (-gim).astype(BF16)
    gx[0, :NX, :NX] = gre
    gx[0, :NX, NX:] = gim
    gx[0, NX:, :NX] = ngim
    gx[0, NX:, NX:] = gre
    gx[1, :NX, :NX] = gre
    gx[1, :NX, NX:] = ngim
    gx[1, NX:, :NX] = gim
    gx[1, NX:, NX:] = gre
    save_gx.start()
    re, im = unit_parts(lax.broadcasted_iota(jnp.int32, (NY, KR), 0) * ky_row)
    ft[0, :, :KR] = re.astype(BF16)
    ft[0, :, KR:] = im.astype(BF16)
    ft[1, :, :KR] = (-im).astype(BF16)
    ft[1, :, KR:] = re.astype(BF16)
    ky_wide = jnp.concatenate([ky_col, ky_col], axis=1)
    re, im = unit_parts(ky_wide * lax.broadcasted_iota(jnp.int32, (KR, NY), 1))
    e[0, :KR] = re.astype(BF16)
    e[0, KR:] = im.astype(BF16)
    e[1, :KR] = (-im).astype(BF16)
    e[1, KR:] = re.astype(BF16)
    cy = (((ky_wide + 128) & 255) - 128).astype(F32) * F32(1.0 / 128.0)
    cx_index = lax.broadcasted_iota(jnp.int32, (KR, NX), 1)
    cx = (((cx_index + 128) & 255) - 128).astype(F32) * F32(1.0 / 128.0)
    elapsed = jnp.sqrt(cy * cy + cx * cx)
    image_row = lax.broadcasted_iota(jnp.int32, (NY, KR), 0)

    def saves(slot):
        return (
            pltpu.make_async_copy(g.at[slot], g_out.at[slot], g_sem.at[slot]),
            pltpu.make_async_copy(gt.at[slot], gt_out.at[slot], gt_sem.at[slot]),
            pltpu.make_async_copy(turn.at[slot], turn_out.at[slot], turn_sem.at[slot]),
        )

    @pl.loop(0, NSEG)
    def _(slot):
        seg = segment_of(slot)
        s, c = sin_cos(freq_ref[seg] * elapsed)
        turn[slot, 0] = c
        turn[slot, 1] = s
        bands = [bands_ref[block_of(t), seg] for t in range(OT)]
        yr_row = spread(bands, lax.broadcasted_iota(jnp.int32, (8, KR), 1), BR)[:1]
        pick = jnp.where(image_row == yr_row, F32(1), F32(0)).astype(BF16)
        g[slot, :, :KR] = mm(e[0], pick).astype(BF16)
        g[slot, :, KR:] = mm(e[1], pick).astype(BF16)
        for t in range(OT):
            at = pl.ds(pl.multiple_of(bands[t] * BR, BR), BR)
            gt[slot, t * BR : (t + 1) * BR] = ft[0, at]
            gt[slot, KR + t * BR : KR + (t + 1) * BR] = ft[1, at]
        for copy in saves(slot):
            copy.start()

    @pl.loop(0, NSEG)
    def _(slot):
        for copy in saves(slot):
            copy.wait()

    save_gx.wait()


def mm(a, b):
    return jnp.dot(a, b, preferred_element_type=F32)


def normal_kernel(
    bands_ref, count_ref, p_ref, sens_in, w_in, g_in, h1_in, o1_in, h2_in, o2_in, h3_in, o3_in,
    gx_in, turn_in, gt_in, out_ref,
    coil, blk, first, ks, acc, mine, own, far, g, gx, turn, gt, sem,
):
    y = lax.axis_index("segments")
    plane = lax.rem(y, 2)
    pieces = [(sens_in.at[y // 2, plane], mine), (w_in.at[:, :, plane], own), (g_in.at[:SEGS_DEV], g.at[:SEGS_DEV])]
    pieces += [(g_in.at[SEGS_DEV:], g.at[SEGS_DEV:])]
    pieces += [(half, far.at[i]) for i, half in enumerate((h1_in, o1_in, h2_in, o2_in, h3_in, o3_in))]
    pieces += [(gx_in, gx), (turn_in, turn), (gt_in, gt)]
    loads = [pltpu.make_async_copy(source, target, sem.at[i]) for i, (source, target) in enumerate(pieces)]
    for load in loads:
        load.start()
    loads[0].wait()

    def weight(slot, t, seg):
        k, i = slot // SEGS_DEV, slot % SEGS_DEV
        j = block_of(t)
        live = (j < count_ref[seg]).astype(F32)
        if k == 0:
            w = own[i, j]
        else:
            w = far[2 * (k - 1) + t // HALF, i, t % HALF]
        at = pl.ds(pl.multiple_of(bands_ref[j, seg] * BR, BR), BR)
        return w.astype(F32) * live, at

    sre = mine[0].astype(F32)
    sim = mine[1].astype(F32)
    p = p_ref[...].astype(jnp.int32).astype(F32) * F32(1.0 / CODE)
    pre = p[:, :ROWS].reshape(NY, NX)
    pim = p[:, ROWS:].reshape(NY, NX)
    coil[0] = sre * pre - sim * pim
    coil[1] = sre * pim + sim * pre
    acc[...] = jnp.zeros_like(acc)
    for slot in range(NSEG):
        seg = segment_of(slot)
        if slot == 0:
            loads[1].wait()
            loads[2].wait()
        elif slot % SEGS_DEV == 0:
            k = slot // SEGS_DEV
            if k == 1:
                loads[3].wait()
            loads[2 * k + 2].wait()
            loads[2 * k + 3].wait()
        for t in range(OT):
            w, at = weight(slot, t, seg)
            blk[slot % 2, t * BR : (t + 1) * BR] = (coil[0, at] * w).astype(BF16)
            blk[slot % 2, KR + t * BR : KR + (t + 1) * BR] = (coil[1, at] * w).astype(BF16)
        got = mm(g[slot], blk[slot % 2]).astype(BF16)
        first[slot * KR : (slot + 1) * KR, :NX] = got[:KR]
        first[slot * KR : (slot + 1) * KR, NX:] = got[KR:]
    loads[10].wait()
    loads[11].wait()
    for pair in range(NSEG // 2):
        spec = mm(first[pair * 2 * KR : (pair + 1) * 2 * KR], gx[0])
        tre, tim = 0.0, 0.0
        for half in range(2):
            re, im = spec[half * KR : (half + 1) * KR, :NX], spec[half * KR : (half + 1) * KR, NX:]
            c, s = turn[pair * 2 + half, 0], turn[pair * 2 + half, 1]
            tre = tre + (re * c + im * s)
            tim = tim + (im * c - re * s)
        if pair == 0:
            ks[:, :NX] = tre
            ks[:, NX:] = tim
        else:
            ks[:, :NX] += tre
            ks[:, NX:] += tim
    loads[12].wait()
    for pair in range(NSEG // 2):
        for half in range(2):
            re, im = ks[:, :NX], ks[:, NX:]
            c, s = turn[pair * 2 + half, 0], turn[pair * 2 + half, 1]
            here = slice((pair * 2 + half) * KR, (pair * 2 + half + 1) * KR)
            first[here, :NX] = (re * c - im * s).astype(BF16)
            first[here, NX:] = (im * c + re * s).astype(BF16)
        back = mm(first[pair * 2 * KR : (pair + 1) * 2 * KR], gx[1]).astype(BF16)
        for half in range(2):
            slot = pair * 2 + half
            seg = segment_of(slot)
            mid = back[half * KR : (half + 1) * KR]
            band = mm(gt[slot], jnp.concatenate([mid[:, :NX], mid[:, NX:]], axis=0))
            for t in range(OT):
                w, at = weight(slot, t, seg)
                acc[0, at] += band[t * BR : (t + 1) * BR] * w
                acc[1, at] += band[KR + t * BR : KR + (t + 1) * BR] * w
    sre = mine[0].astype(F32)
    sim = mine[1].astype(F32)
    out_re = (sre * acc[0] + sim * acc[1]).reshape(GROUP, ROWS, NX)
    out_im = (sre * acc[1] - sim * acc[0]).reshape(GROUP, ROWS, NX)
    out_ref[...] = jnp.concatenate([out_re, out_im], axis=1).astype(BF16)


def applied_kernel(parts_ref, r_ref, p_ref, low_ref, high_ref, applied_ref, sums_ref):
    totals = [jnp.zeros((ROWS, NX), F32) for _ in range(4)]
    for q in range(2):
        total = jnp.zeros((2 * ROWS, NX), F32)
        for pair in range(2):
            for xc in range(8):
                total = total + parts_ref[(pair * 2 + q) * 8 + xc].astype(F32)
        for c in range(2):
            p = p_ref[0, q, c]
            r = r_ref[0, q, c]
            smooth = 2.0 * p - low_ref[0, q, c].astype(F32) - high_ref[0, q, c].astype(F32)
            applied = total[c * ROWS : (c + 1) * ROWS] + reg_weight * smooth + shift_weight * p
            applied_ref[0, q, c] = applied
            for i, term in enumerate((r * r, p * applied, r * applied, applied * applied)):
                totals[i] = totals[i] + term
    lane = lax.broadcasted_iota(jnp.int32, (8, 128), 1)
    line = jnp.zeros((8, 128), F32)
    for i in range(4):
        whole = jnp.sum(jnp.sum(totals[i], axis=0, keepdims=True), axis=1, keepdims=True)
        line = jnp.where(lane == i, whole, line)
    sums_ref[...] = jnp.broadcast_to(line[:1, :8], (DEVICES, 8))


def update_kernel(sums_ref, x_ref, r_ref, p_ref, applied_ref, x_out, r_out, p_out):
    sums = jnp.sum(sums_ref[...], axis=0, keepdims=True)
    rr, pa, ra, aa = (sums[:, i : i + 1] for i in range(4))
    alpha = rr / (pa + epsilon)
    rnew = rr - 2.0 * alpha * ra + alpha * alpha * aa
    beta = rnew / (rr + epsilon)
    alpha = jnp.broadcast_to(alpha, (ROWS, NX))
    beta = jnp.broadcast_to(beta, (ROWS, NX))
    for q in range(2):
        for c in range(2):
            p = p_ref[0, q, c]
            r = r_ref[0, q, c] - alpha * applied_ref[0, q, c]
            x_out[0, q, c] = x_ref[0, q, c] + alpha * p
            r_out[0, q, c] = r
            p_out[0, q, c] = r + beta * p


VM = pl.BlockSpec(memory_space=pltpu.VMEM)
SM = pl.BlockSpec(memory_space=pltpu.SMEM)
HB = pl.BlockSpec(memory_space=pltpu.HBM)


def hbm(array):
    return pltpu.with_memory_space_constraint(array, pltpu.HBM)


def local(x_in, r_in, p_in, sens, seg_weights, seg_freq, band_ids, seg_count, k_bands):
    half_shape = jax.ShapeDtypeStruct((SEGS_DEV, HALF, BR, NX), BF16)
    send, same, other = pl.pallas_call(
        prep_kernel,
        in_specs=[VM, VM],
        out_specs=[VM, VM, VM],
        out_shape=[jax.ShapeDtypeStruct((GROUP, 2 * ROWS, NX), jnp.int16), half_shape, half_shape],
        compiler_params=pltpu.CompilerParams(vmem_limit_bytes=4 << 20),
        name="prep",
    )(hbm(p_in), hbm(seg_weights))
    halves = [
        lax.ppermute(same if k == 2 else other, "segments", [(i, (i + k) % 4) for i in range(4)])
        for k in (1, 2, 3)
    ]
    whole = lax.all_to_all(send, SPACE, 0, 0, tiled=True)
    halo = p_in.astype(BF16)
    low = lax.ppermute(halo, "frames", [(i, (i + 1) % 8) for i in range(8)])
    high = lax.ppermute(halo, "frames", [(i, (i + 7) % 8) for i in range(8)])
    bands = hbm(band_ids.T)
    g, gt, gx, turn = pl.pallas_call(
        tables_kernel,
        in_specs=[SM, SM, SM],
        out_specs=[HB] * 4,
        out_shape=[
            pltpu.HBM((NSEG, 2 * KR, 2 * KR), BF16),
            pltpu.HBM((NSEG, 2 * KR, 2 * KR), BF16),
            pltpu.HBM((2, 2 * NX, 2 * NX), BF16),
            pltpu.HBM((NSEG, 2, KR, NX), F32),
        ],
        scratch_shapes=[
            pltpu.VMEM((NSEG, 2 * KR, 2 * KR), BF16),
            pltpu.VMEM((NSEG, 2 * KR, 2 * KR), BF16),
            pltpu.VMEM((2, 2 * NX, 2 * NX), BF16),
            pltpu.VMEM((NSEG, 2, KR, NX), F32),
            pltpu.VMEM((2, NY, 2 * KR), BF16),
            pltpu.VMEM((2, 2 * KR, NY), BF16),
            pltpu.SemaphoreType.DMA((NSEG,)),
            pltpu.SemaphoreType.DMA((NSEG,)),
            pltpu.SemaphoreType.DMA((NSEG,)),
            pltpu.SemaphoreType.DMA((1,)),
        ],
        compiler_params=pltpu.CompilerParams(vmem_limit_bytes=32 << 20),
        cost_estimate=pl.CostEstimate(flops=30_000_000, bytes_accessed=8 << 20, transcendentals=0),
        name="tables",
    )(bands, hbm(k_bands), hbm(seg_freq))
    halves, g = lax.optimization_barrier((halves, g))
    others = [lax.ppermute(half, "coils", [(i, i ^ 1) for i in range(8)]) for half in halves]
    parts = pl.pallas_call(
        normal_kernel,
        in_specs=[SM, SM, VM] + [HB] * 12,
        out_specs=VM,
        out_shape=jax.ShapeDtypeStruct((GROUP, 2 * ROWS, NX), BF16),
        scratch_shapes=[
            pltpu.VMEM((2, NY, NX), F32),
            pltpu.VMEM((2, 2 * KR, NX), BF16),
            pltpu.VMEM((NSEG * KR, 2 * NX), BF16),
            pltpu.VMEM((KR, 2 * NX), F32),
            pltpu.VMEM((2, NY, NX), F32),
            pltpu.VMEM((2, NY, NX), BF16),
            pltpu.VMEM((SEGS_DEV, OT, BR, NX), BF16),
            pltpu.VMEM((6, SEGS_DEV, HALF, BR, NX), BF16),
            pltpu.VMEM((NSEG, 2 * KR, 2 * KR), BF16),
            pltpu.VMEM((2, 2 * NX, 2 * NX), BF16),
            pltpu.VMEM((NSEG, 2, KR, NX), F32),
            pltpu.VMEM((NSEG, 2 * KR, 2 * KR), BF16),
            pltpu.SemaphoreType.DMA((13,)),
        ],
        compiler_params=pltpu.CompilerParams(vmem_limit_bytes=32 << 20),
        cost_estimate=pl.CostEstimate(flops=2_400_000_000, bytes_accessed=8 << 20, transcendentals=0),
        name="normal",
    )(
        bands, hbm(seg_count), whole, hbm(sens), hbm(seg_weights), hbm(g),
        *map(hbm, (halves[0], others[0], halves[1], others[1], halves[2], others[2])), hbm(gx), hbm(turn), hbm(gt),
    )
    parts = lax.all_to_all(parts, SPACE, 0, 0, tiled=True)
    share = jax.ShapeDtypeStruct(p_in.shape, F32)
    applied, sums = pl.pallas_call(
        applied_kernel,
        in_specs=[VM] * 5,
        out_specs=[VM, VM],
        out_shape=[share, jax.ShapeDtypeStruct((DEVICES, 8), F32)],
        compiler_params=pltpu.CompilerParams(vmem_limit_bytes=4 << 20),
        name="applied",
    )(parts, r_in, p_in, low, high)
    sums = lax.all_to_all(sums, ("frames", "segments", "coils"), 0, 0, tiled=True)
    return tuple(
        pl.pallas_call(
            update_kernel,
            in_specs=[VM] * 5,
            out_specs=[VM] * 3,
            out_shape=[share] * 3,
            compiler_params=pltpu.CompilerParams(vmem_limit_bytes=4 << 20),
            name="update",
        )(sums, x_in, r_in, p_in, applied)
    )


def solution(mesh):
    image = P("frames", None, None, ("segments", "coils"), None)
    in_specs = (
        image,
        image,
        image,
        P("coils", None, None, None, None),
        P("segments", None, None, None, None),
        P(),
        P(),
        P(),
        P("frames", None),
    )
    return jax.shard_map(local, mesh=mesh, in_specs=in_specs, out_specs=(image,) * 3, check_vma=False)
```

```python
import math

import jax
import jax.numpy as jnp
from jax import lax
from jax.experimental import pallas as pl
from jax.experimental.pallas import tpu as pltpu
from jax.sharding import PartitionSpec as P

BR = 16
KB = 8
NX = 256
NY = 256
OT = 8
NSEG = 12
KR = 128
SEGS_DEV = 3
YDEV = 4
GROUP = 32
ROWS = 8
HALF = OT // 2
DEVICES = 256
CODE = 32767.0 / 6.0

reg_weight = 0.5
shift_weight = 0.1
epsilon = 1e-06

F32 = jnp.float32
BF16 = jnp.bfloat16
SPACE = ("segments", "coils")


def sin_cos(angle):
    half = angle * 0.5
    sq = half * half
    s = F32(1.0 / math.factorial(13))
    for n in (11, 9, 7, 5, 3, 1):
        s = s * sq + F32((-1.0) ** (n // 2) / math.factorial(n))
    s = s * half
    c = F32(1.0 / math.factorial(16))
    for n in (14, 12, 10, 8, 6, 4, 2, 0):
        c = c * sq + F32((-1.0) ** (n // 2) / math.factorial(n))
    return 2.0 * s * c, 1.0 - 2.0 * s * s


def unit_parts(products):
    n = ((products + 128) & 255) - 128
    s, c = sin_cos(n.astype(F32) * F32(2.0 * math.pi / 256))
    return c * F32(1.0 / 16.0), s * F32(-1.0 / 16.0)


def segment_of(slot):
    y = lax.axis_index("segments")
    return lax.rem(y - slot // SEGS_DEV + YDEV, YDEV) * SEGS_DEV + slot % SEGS_DEV


def block_of(place):
    core = lax.rem(lax.axis_index("coils"), 2)
    return lax.rem(core * HALF + place, OT)


def spread(values, index, width):
    out = jnp.zeros_like(index)
    for j, value in enumerate(values):
        out = jnp.where(index // width == j, value * width + index % width, out)
    return out


def prep_kernel(p_ref, w_ref, send_ref, same_ref, other_ref):
    plane = lax.rem(lax.axis_index("segments"), 2)
    core = lax.rem(lax.axis_index("coils"), 2)
    for i in range(SEGS_DEV):
        for t in range(HALF):
            same_ref[i, t] = w_ref[i, core * HALF + t, plane]
            other_ref[i, t] = w_ref[i, core * HALF + t, 1 - plane]
    for q in range(2):
        both = jnp.concatenate([p_ref[0, q, 0], p_ref[0, q, 1]], axis=0)
        code = jnp.floor(both * F32(CODE) + 0.5).astype(jnp.int32).astype(jnp.int16)
        for pair in range(2):
            for xc in range(8):
                send_ref[(pair * 2 + q) * 8 + xc] = code


def turns_kernel(kb_ref, freq_ref, h1, h2, h3, turn_out, turn, turn_sem):
    kbs = [kb_ref[0, j] for j in range(KR // KB)]
    ky = spread(kbs, lax.broadcasted_iota(jnp.int32, (KR, KR), 0), KB)
    cy = (((ky + 128) & 255) - 128).astype(F32) * F32(1.0 / 128.0)
    cy = jnp.concatenate([cy, cy], axis=1)
    cx_index = lax.broadcasted_iota(jnp.int32, (KR, NX), 1)
    cx = (((cx_index + 128) & 255) - 128).astype(F32) * F32(1.0 / 128.0)
    elapsed = jnp.sqrt(cy * cy + cx * cx)
    saves = [pltpu.make_async_copy(turn.at[slot], turn_out.at[slot], turn_sem.at[slot]) for slot in range(NSEG)]
    for slot in range(NSEG):
        turn[slot, 1], turn[slot, 0] = sin_cos(freq_ref[segment_of(slot)] * elapsed)
        saves[slot].start()
    for save in saves:
        save.wait()


def tables_kernel(bands_ref, kb_ref, g_ref, ft, gx_ref, e):
    kbs = [kb_ref[0, j] for j in range(KR // KB)]
    ky_col = spread(kbs, lax.broadcasted_iota(jnp.int32, (KR, KR), 0), KB)
    ky_row = spread(kbs, lax.broadcasted_iota(jnp.int32, (8, KR), 1), KB)[:1]
    ky_wide = jnp.concatenate([ky_col, ky_col], axis=1)
    rows = lax.broadcasted_iota(jnp.int32, (NX, NX), 0)
    cols = lax.broadcasted_iota(jnp.int32, (NX, NX), 1)
    re, im = unit_parts(rows * cols)
    gx_ref[0] = re.astype(BF16)
    gx_ref[1] = im.astype(BF16)
    re, im = unit_parts(lax.broadcasted_iota(jnp.int32, (NY, KR), 0) * ky_row)
    ft[0, :, :KR] = re.astype(BF16)
    ft[0, :, KR:] = im.astype(BF16)
    ft[1, :, :KR] = (-im).astype(BF16)
    ft[1, :, KR:] = re.astype(BF16)
    re, im = unit_parts(ky_wide * lax.broadcasted_iota(jnp.int32, (KR, NY), 1))
    e[0, :KR] = re.astype(BF16)
    e[0, KR:] = im.astype(BF16)
    e[1, :KR] = (-im).astype(BF16)
    e[1, KR:] = re.astype(BF16)
    image_row = lax.broadcasted_iota(jnp.int32, (NY, KR), 0)
    for slot in range(NSEG):
        seg = segment_of(slot)
        bands = [bands_ref[block_of(t), seg] for t in range(OT)]
        yr_row = spread(bands, lax.broadcasted_iota(jnp.int32, (8, KR), 1), BR)[:1]
        pick = jnp.where(image_row == yr_row, F32(1), F32(0)).astype(BF16)
        g_ref[slot, :, :KR] = mm(e[0], pick).astype(BF16)
        g_ref[slot, :, KR:] = mm(e[1], pick).astype(BF16)


def mm(a, b):
    return jnp.dot(a, b, preferred_element_type=F32)


def normal_kernel(
    bands_ref, count_ref, p_ref, g, ft, gx_ref, h1, o1, h2, o2, h3, o3, sens_in, w_in, turn_in, out_ref,
    coil, blk, first, ks, acc, mine, near, gx, turn, sem,
):
    y = lax.axis_index("segments")
    plane = lax.rem(y, 2)
    core = lax.rem(lax.axis_index("coils"), 2)
    loads = [
        pltpu.make_async_copy(source, target, sem.at[i])
        for i, (source, target) in enumerate(
            [
                (sens_in.at[y // 2, plane], mine),
                (w_in.at[:, pl.ds(core * HALF, HALF), plane], near.at[0]),
                (w_in.at[:, pl.ds((1 - core) * HALF, HALF), plane], near.at[1]),
                (turn_in, turn),
            ]
        )
    ]
    for load in loads:
        load.start()
    halves = ((near.at[0], near.at[1]), (h1, o1), (h2, o2), (h3, o3))
    gre, gim = gx_ref[0], gx_ref[1]
    for i, sign in enumerate((1, -1)):
        gx[i, :NX, :NX] = gre
        gx[i, :NX, NX:] = sign * gim
        gx[i, NX:, :NX] = -sign * gim
        gx[i, NX:, NX:] = gre

    def weight(slot, t):
        seg = segment_of(slot)
        j = block_of(t)
        live = (j < count_ref[seg]).astype(F32)
        w = halves[slot // SEGS_DEV][t // HALF][slot % SEGS_DEV, t % HALF]
        at = pl.ds(pl.multiple_of(bands_ref[j, seg] * BR, BR), BR)
        return w.astype(F32) * live, at

    loads[0].wait()
    for chunk in range(4):
        rows = slice(chunk * 64, chunk * 64 + 64)
        p = p_ref[chunk * 8 : chunk * 8 + 8].astype(jnp.int32).astype(F32) * F32(1.0 / CODE)
        pre = p[:, :ROWS].reshape(64, NX)
        pim = p[:, ROWS:].reshape(64, NX)
        sre = mine[0, rows].astype(F32)
        sim = mine[1, rows].astype(F32)
        coil[0, rows] = sre * pre - sim * pim
        coil[1, rows] = sre * pim + sim * pre
    acc[...] = jnp.zeros_like(acc)
    loads[1].wait()
    loads[2].wait()
    for slot in range(NSEG):
        for t in range(OT):
            w, at = weight(slot, t)
            blk[slot, t * BR : (t + 1) * BR] = (coil[0, at] * w).astype(BF16)
            blk[slot, KR + t * BR : KR + (t + 1) * BR] = (coil[1, at] * w).astype(BF16)
        got = mm(g[slot], blk[slot]).astype(BF16)
        first[slot * KR : (slot + 1) * KR, :NX] = got[:KR]
        first[slot * KR : (slot + 1) * KR, NX:] = got[KR:]
    loads[3].wait()
    for pair in range(NSEG // 2):
        spec = mm(first[pair * 2 * KR : (pair + 1) * 2 * KR], gx[0])
        tre, tim = 0.0, 0.0
        for half in range(2):
            re, im = spec[half * KR : (half + 1) * KR, :NX], spec[half * KR : (half + 1) * KR, NX:]
            c, s = turn[pair * 2 + half, 0], turn[pair * 2 + half, 1]
            tre = tre + (re * c + im * s)
            tim = tim + (im * c - re * s)
        ks[0] = tre if pair == 0 else ks[0] + tre
        ks[1] = tim if pair == 0 else ks[1] + tim
    for pair in range(NSEG // 2):
        for half in range(2):
            re, im = ks[0], ks[1]
            c, s = turn[pair * 2 + half, 0], turn[pair * 2 + half, 1]
            here = slice((pair * 2 + half) * KR, (pair * 2 + half + 1) * KR)
            first[here, :NX] = (re * c - im * s).astype(BF16)
            first[here, NX:] = (im * c + re * s).astype(BF16)
        back = mm(first[pair * 2 * KR : (pair + 1) * 2 * KR], gx[1]).astype(BF16)
        for half in range(2):
            slot = pair * 2 + half
            places = [weight(slot, t) for t in range(OT)]
            rows = jnp.concatenate([ft[c, at] for c in range(2) for _, at in places], axis=0)
            mid = back[half * KR : (half + 1) * KR]
            band = mm(rows, jnp.concatenate([mid[:, :NX], mid[:, NX:]], axis=0))
            for t, (w, at) in enumerate(places):
                acc[0, at] += band[t * BR : (t + 1) * BR] * w
                acc[1, at] += band[KR + t * BR : KR + (t + 1) * BR] * w
    for chunk in range(4):
        rows = slice(chunk * 64, chunk * 64 + 64)
        sre = mine[0, rows].astype(F32)
        sim = mine[1, rows].astype(F32)
        are, aim = acc[0, rows], acc[1, rows]
        out_re = (sre * are + sim * aim).reshape(8, ROWS, NX)
        out_im = (sre * aim - sim * are).reshape(8, ROWS, NX)
        out_ref[chunk * 8 : chunk * 8 + 8] = jnp.concatenate([out_re, out_im], axis=1).astype(BF16)


def applied_kernel(parts_ref, r_ref, p_ref, low_ref, high_ref, applied_ref, sums_ref):
    totals = [jnp.zeros((ROWS, NX), F32) for _ in range(4)]
    for q in range(2):
        total = jnp.zeros((2 * ROWS, NX), F32)
        for pair in range(2):
            for xc in range(8):
                total = total + parts_ref[(pair * 2 + q) * 8 + xc].astype(F32)
        for c in range(2):
            p = p_ref[0, q, c]
            r = r_ref[0, q, c]
            smooth = 2.0 * p - low_ref[0, q, c].astype(F32) - high_ref[0, q, c].astype(F32)
            applied = total[c * ROWS : (c + 1) * ROWS] + reg_weight * smooth + shift_weight * p
            applied_ref[0, q, c] = applied
            for i, term in enumerate((r * r, p * applied, r * applied, applied * applied)):
                totals[i] = totals[i] + term
    lane = lax.broadcasted_iota(jnp.int32, (8, 128), 1)
    line = jnp.zeros((8, 128), F32)
    for i in range(4):
        whole = jnp.sum(jnp.sum(totals[i], axis=0, keepdims=True), axis=1, keepdims=True)
        line = jnp.where(lane == i, whole, line)
    sums_ref[...] = jnp.broadcast_to(line[:1, :8], (DEVICES, 8))


def update_kernel(sums_ref, x_ref, r_ref, p_ref, applied_ref, x_out, r_out, p_out):
    sums = jnp.sum(sums_ref[...], axis=0, keepdims=True)
    rr, pa, ra, aa = (sums[:, i : i + 1] for i in range(4))
    alpha = rr / (pa + epsilon)
    rnew = rr - 2.0 * alpha * ra + alpha * alpha * aa
    beta = rnew / (rr + epsilon)
    alpha = jnp.broadcast_to(alpha, (ROWS, NX))
    beta = jnp.broadcast_to(beta, (ROWS, NX))
    for q in range(2):
        for c in range(2):
            p = p_ref[0, q, c]
            r = r_ref[0, q, c] - alpha * applied_ref[0, q, c]
            x_out[0, q, c] = x_ref[0, q, c] + alpha * p
            r_out[0, q, c] = r
            p_out[0, q, c] = r + beta * p


VM = pl.BlockSpec(memory_space=pltpu.VMEM)
SM = pl.BlockSpec(memory_space=pltpu.SMEM)
HB = pl.BlockSpec(memory_space=pltpu.HBM)


def hbm(array):
    return pltpu.with_memory_space_constraint(array, pltpu.HBM)


def local(x_in, r_in, p_in, sens, seg_weights, seg_freq, band_ids, seg_count, k_bands):
    half_shape = jax.ShapeDtypeStruct((SEGS_DEV, HALF, BR, NX), BF16)
    send, same, other = pl.pallas_call(
        prep_kernel,
        in_specs=[VM, VM],
        out_specs=[VM, VM, VM],
        out_shape=[jax.ShapeDtypeStruct((GROUP, 2 * ROWS, NX), jnp.int16), half_shape, half_shape],
        compiler_params=pltpu.CompilerParams(vmem_limit_bytes=4 << 20),
        name="prep",
    )(hbm(p_in), hbm(seg_weights))
    halves = [
        lax.ppermute(same if k == 2 else other, "segments", [(i, (i + k) % 4) for i in range(4)])
        for k in (1, 2, 3)
    ]
    whole = lax.all_to_all(send, SPACE, 0, 0, tiled=True)
    halo = p_in.astype(BF16)
    low = lax.ppermute(halo, "frames", [(i, (i + 1) % 8) for i in range(8)])
    high = lax.ppermute(halo, "frames", [(i, (i + 7) % 8) for i in range(8)])
    bands = hbm(band_ids.T)
    g, ft, gx = pl.pallas_call(
        tables_kernel,
        in_specs=[SM, SM],
        out_specs=[VM, VM, VM],
        out_shape=[
            jax.ShapeDtypeStruct((NSEG, 2 * KR, 2 * KR), BF16),
            jax.ShapeDtypeStruct((2, NY, 2 * KR), BF16),
            jax.ShapeDtypeStruct((2, NX, NX), BF16),
        ],
        scratch_shapes=[pltpu.VMEM((2, 2 * KR, NY), BF16)],
        compiler_params=pltpu.CompilerParams(vmem_limit_bytes=32 << 20),
        cost_estimate=pl.CostEstimate(flops=1_000_000_000, bytes_accessed=2 << 20, transcendentals=0),
        name="tables",
    )(bands, hbm(k_bands))
    turn = pl.pallas_call(
        turns_kernel,
        in_specs=[SM, SM] + [pl.BlockSpec(memory_space=pl.ANY)] * 3,
        out_specs=HB,
        out_shape=pltpu.HBM((NSEG, 2, KR, NX), F32),
        scratch_shapes=[pltpu.VMEM((NSEG, 2, KR, NX), F32), pltpu.SemaphoreType.DMA((NSEG,))],
        compiler_params=pltpu.CompilerParams(vmem_limit_bytes=32 << 20),
        cost_estimate=pl.CostEstimate(flops=40_000_000_000, bytes_accessed=3 << 20, transcendentals=0),
        name="turns",
    )(hbm(k_bands), hbm(seg_freq), *halves)
    others = [lax.ppermute(half, "coils", [(i, i ^ 1) for i in range(8)]) for half in halves]
    parts = pl.pallas_call(
        normal_kernel,
        in_specs=[SM] * 2 + [VM] * 10 + [HB] * 3,
        out_specs=VM,
        out_shape=jax.ShapeDtypeStruct((GROUP, 2 * ROWS, NX), BF16),
        scratch_shapes=[
            pltpu.VMEM((2, NY, NX), F32),
            pltpu.VMEM((NSEG, 2 * KR, NX), BF16),
            pltpu.VMEM((NSEG * KR, 2 * NX), BF16),
            pltpu.VMEM((2, KR, NX), F32),
            pltpu.VMEM((2, NY, NX), F32),
            pltpu.VMEM((2, NY, NX), BF16),
            pltpu.VMEM((2, SEGS_DEV, HALF, BR, NX), BF16),
            pltpu.VMEM((2, 2 * NX, 2 * NX), BF16),
            pltpu.VMEM((NSEG, 2, KR, NX), F32),
            pltpu.SemaphoreType.DMA((4,)),
        ],
        compiler_params=pltpu.CompilerParams(vmem_limit_bytes=32 << 20),
        cost_estimate=pl.CostEstimate(flops=2_400_000_000, bytes_accessed=8 << 20, transcendentals=0),
        name="normal",
    )(
        bands, hbm(seg_count), whole, g, ft, gx,
        halves[0], others[0], halves[1], others[1], halves[2], others[2], hbm(sens), hbm(seg_weights), hbm(turn),
    )
    parts = lax.all_to_all(parts, SPACE, 0, 0, tiled=True)
    share = jax.ShapeDtypeStruct(p_in.shape, F32)
    applied, sums = pl.pallas_call(
        applied_kernel,
        in_specs=[VM] * 5,
        out_specs=[VM, VM],
        out_shape=[share, jax.ShapeDtypeStruct((DEVICES, 8), F32)],
        compiler_params=pltpu.CompilerParams(vmem_limit_bytes=4 << 20),
        name="applied",
    )(parts, r_in, p_in, low, high)
    sums = lax.all_to_all(sums, ("frames", "segments", "coils"), 0, 0, tiled=True)
    return tuple(
        pl.pallas_call(
            update_kernel,
            in_specs=[VM] * 5,
            out_specs=[VM] * 3,
            out_shape=[share] * 3,
            compiler_params=pltpu.CompilerParams(vmem_limit_bytes=4 << 20),
            name="update",
        )(sums, x_in, r_in, p_in, applied)
    )


def solution(mesh):
    image = P("frames", None, None, ("segments", "coils"), None)
    in_specs = (
        image,
        image,
        image,
        P("coils", None, None, None, None),
        P("segments", None, None, None, None),
        P(),
        P(),
        P(),
        P("frames", None),
    )
    return jax.shard_map(local, mesh=mesh, in_specs=in_specs, out_specs=(image,) * 3, check_vma=False)
```

```python
import math

import jax
import jax.numpy as jnp
from jax import lax
from jax.experimental import pallas as pl
from jax.experimental.pallas import tpu as pltpu
from jax.sharding import PartitionSpec as P

BR = 16
KB = 8
NX = 256
NY = 256
OT = 8
NSEG = 12
KR = 128
SEGS_DEV = 3
YDEV = 4
GROUP = 32
ROWS = 8
HALF = OT // 2
DEVICES = 256
CODE = 32767.0 / 6.0

reg_weight = 0.5
shift_weight = 0.1
epsilon = 1e-06

F32 = jnp.float32
BF16 = jnp.bfloat16
SPACE = ("segments", "coils")


def sin_cos(quarter):
    sq = quarter * quarter
    s = F32(1.0 / math.factorial(9))
    for n in (7, 5, 3, 1):
        s = s * sq + F32((-1.0) ** (n // 2) / math.factorial(n))
    s = s * quarter
    c = F32(-1.0 / math.factorial(10))
    for n in (8, 6, 4, 2, 0):
        c = c * sq + F32((-1.0) ** (n // 2) / math.factorial(n))
    twice = s + s
    s, c = twice * c, 1.0 - twice * s
    twice = s + s
    return twice * c, 1.0 - twice * s


def unit_parts(products):
    n = ((products + 128) & 255) - 128
    s, c = sin_cos(n.astype(F32) * F32(0.5 * math.pi / 256))
    return c * F32(1.0 / 16.0), s * F32(-1.0 / 16.0)


def segment_of(slot):
    y = lax.axis_index("segments")
    return lax.rem(y - slot // SEGS_DEV + YDEV, YDEV) * SEGS_DEV + slot % SEGS_DEV


def block_of(place):
    core = lax.rem(lax.axis_index("coils"), 2)
    return lax.rem(core * HALF + place, OT)


def spread(values, index, width):
    out = jnp.zeros_like(index)
    for j, value in enumerate(values):
        out = jnp.where(index // width == j, value * width + index % width, out)
    return out


def prep_kernel(p_ref, w_ref, send_ref, same_ref, other_ref):
    plane = lax.rem(lax.axis_index("segments"), 2)
    core = lax.rem(lax.axis_index("coils"), 2)
    for i in range(SEGS_DEV):
        for t in range(HALF):
            same_ref[i, t] = w_ref[i, core * HALF + t, plane]
            other_ref[i, t] = w_ref[i, core * HALF + t, 1 - plane]
    for q in range(2):
        both = jnp.concatenate([p_ref[0, q, 0], p_ref[0, q, 1]], axis=0)
        code = jnp.floor(both * F32(CODE) + 0.5).astype(jnp.int32).astype(jnp.int16)
        for pair in range(2):
            for xc in range(8):
                send_ref[(pair * 2 + q) * 8 + xc] = code


def turns_kernel(elapsed_ref, freq_ref, h1, h2, h3, turn_out, turn, turn_sem):
    saves = [pltpu.make_async_copy(turn.at[slot], turn_out.at[slot], turn_sem.at[slot]) for slot in range(NSEG)]
    for slot in range(NSEG):
        turn[slot, 1], turn[slot, 0] = sin_cos(freq_ref[slot] * elapsed_ref[...])
        saves[slot].start()
    for save in saves:
        save.wait()


def tables_kernel(
    bands_in, kb_in, freq_in, g_ref, ft, gx_ref, elapsed_ref, quarter_ref, e, bands_ref, kb_ref, freq_ref, sem
):
    loads = [
        pltpu.make_async_copy(source, target, sem.at[i])
        for i, (source, target) in enumerate([(bands_in, bands_ref), (kb_in, kb_ref), (freq_in, freq_ref)])
    ]
    for load in loads:
        load.start()
    rows = lax.broadcasted_iota(jnp.int32, (NX, NX), 0)
    cols = lax.broadcasted_iota(jnp.int32, (NX, NX), 1)
    re, im = unit_parts(rows * cols)
    gx_ref[0] = re.astype(BF16)
    gx_ref[1] = im.astype(BF16)
    for load in loads:
        load.wait()
    for slot in range(NSEG):
        quarter_ref[slot] = jnp.broadcast_to(freq_ref[segment_of(slot)] * F32(0.25), (1, NX))
    kbs = [kb_ref[0, j] for j in range(KR // KB)]
    ky_col = spread(kbs, lax.broadcasted_iota(jnp.int32, (KR, KR), 0), KB)
    ky_wide = jnp.concatenate([ky_col, ky_col], axis=1)
    cy = (((ky_wide + 128) & 255) - 128).astype(F32) * F32(1.0 / 128.0)
    cx_index = lax.broadcasted_iota(jnp.int32, (KR, NX), 1)
    cx = (((cx_index + 128) & 255) - 128).astype(F32) * F32(1.0 / 128.0)
    elapsed_ref[...] = jnp.sqrt(cy * cy + cx * cx)
    ky_row = spread(kbs, lax.broadcasted_iota(jnp.int32, (8, KR), 1), KB)[:1]
    re, im = unit_parts(lax.broadcasted_iota(jnp.int32, (NY, KR), 0) * ky_row)
    ft[0, :, :KR] = re.astype(BF16)
    ft[0, :, KR:] = im.astype(BF16)
    ft[1, :, :KR] = (-im).astype(BF16)
    ft[1, :, KR:] = re.astype(BF16)
    re, im = unit_parts(ky_wide * lax.broadcasted_iota(jnp.int32, (KR, NY), 1))
    e[0, :KR] = re.astype(BF16)
    e[0, KR:] = im.astype(BF16)
    e[1, :KR] = (-im).astype(BF16)
    e[1, KR:] = re.astype(BF16)
    image_row = lax.broadcasted_iota(jnp.int32, (NY, KR), 0)
    for slot in range(NSEG):
        seg = segment_of(slot)
        bands = [bands_ref[block_of(t), seg] for t in range(OT)]
        yr_row = spread(bands, lax.broadcasted_iota(jnp.int32, (8, KR), 1), BR)[:1]
        pick = jnp.where(image_row == yr_row, F32(1), F32(0)).astype(BF16)
        g_ref[slot, :, :KR] = mm(e[0], pick).astype(BF16)
        g_ref[slot, :, KR:] = mm(e[1], pick).astype(BF16)


def mm(a, b):
    return jnp.dot(a, b, preferred_element_type=F32)


def normal_kernel(
    bands_in, count_in, p_ref, g, ft, gx_ref, h1, o1, h2, o2, h3, o3, sens_in, w_in, turn_in, out,
    coil, blk, first, ks, acc, mine, near, gx, turn, out_ref, bands_ref, count_ref, sem, out_sem,
):
    y = lax.axis_index("segments")
    plane = lax.rem(y, 2)
    core = lax.rem(lax.axis_index("coils"), 2)
    loads = [
        pltpu.make_async_copy(source, target, sem.at[i])
        for i, (source, target) in enumerate(
            [
                (sens_in.at[y // 2, plane], mine),
                (w_in.at[:, pl.ds(core * HALF, HALF), plane], near.at[0]),
                (w_in.at[:, pl.ds((1 - core) * HALF, HALF), plane], near.at[1]),
                (bands_in, bands_ref),
                (count_in, count_ref),
                (turn_in, turn),
            ]
        )
    ]
    for load in loads:
        load.start()
    halves = ((near.at[0], near.at[1]), (h1, o1), (h2, o2), (h3, o3))
    gre, gim = gx_ref[0], gx_ref[1]
    for i, sign in enumerate((1, -1)):
        gx[i, :NX, :NX] = gre
        gx[i, :NX, NX:] = sign * gim
        gx[i, NX:, :NX] = -sign * gim
        gx[i, NX:, NX:] = gre

    def weight(slot, t):
        seg = segment_of(slot)
        j = block_of(t)
        live = (j < count_ref[seg]).astype(F32)
        w = halves[slot // SEGS_DEV][t // HALF][slot % SEGS_DEV, t % HALF]
        at = pl.ds(pl.multiple_of(bands_ref[j, seg] * BR, BR), BR)
        return w.astype(F32) * live, at

    acc[...] = jnp.zeros_like(acc)
    loads[0].wait()
    for chunk in range(4):
        rows = slice(chunk * 64, chunk * 64 + 64)
        p = p_ref[chunk * 8 : chunk * 8 + 8].astype(jnp.int32).astype(F32) * F32(1.0 / CODE)
        pre = p[:, :ROWS].reshape(64, NX)
        pim = p[:, ROWS:].reshape(64, NX)
        sre = mine[0, rows].astype(F32)
        sim = mine[1, rows].astype(F32)
        coil[0, rows] = sre * pre - sim * pim
        coil[1, rows] = sre * pim + sim * pre
    for load in loads[1:5]:
        load.wait()
    for slot in range(NSEG):
        for t in range(OT):
            w, at = weight(slot, t)
            blk[slot, t * BR : (t + 1) * BR] = (coil[0, at] * w).astype(BF16)
            blk[slot, KR + t * BR : KR + (t + 1) * BR] = (coil[1, at] * w).astype(BF16)
        got = mm(g[slot], blk[slot]).astype(BF16)
        first[slot * KR : (slot + 1) * KR, :NX] = got[:KR]
        first[slot * KR : (slot + 1) * KR, NX:] = got[KR:]
    loads[5].wait()
    for pair in range(NSEG // 2):
        spec = mm(first[pair * 2 * KR : (pair + 1) * 2 * KR], gx[0])
        tre, tim = 0.0, 0.0
        for half in range(2):
            re, im = spec[half * KR : (half + 1) * KR, :NX], spec[half * KR : (half + 1) * KR, NX:]
            c, s = turn[pair * 2 + half, 0], turn[pair * 2 + half, 1]
            tre = tre + (re * c + im * s)
            tim = tim + (im * c - re * s)
        ks[0] = tre if pair == 0 else ks[0] + tre
        ks[1] = tim if pair == 0 else ks[1] + tim
    for pair in range(NSEG // 2):
        for half in range(2):
            re, im = ks[0], ks[1]
            c, s = turn[pair * 2 + half, 0], turn[pair * 2 + half, 1]
            here = slice((pair * 2 + half) * KR, (pair * 2 + half + 1) * KR)
            first[here, :NX] = (re * c - im * s).astype(BF16)
            first[here, NX:] = (im * c + re * s).astype(BF16)
        back = mm(first[pair * 2 * KR : (pair + 1) * 2 * KR], gx[1]).astype(BF16)
        for half in range(2):
            slot = pair * 2 + half
            places = [weight(slot, t) for t in range(OT)]
            rows = jnp.concatenate([ft[c, at] for c in range(2) for _, at in places], axis=0)
            mid = back[half * KR : (half + 1) * KR]
            band = mm(rows, jnp.concatenate([mid[:, :NX], mid[:, NX:]], axis=0))
            for t, (w, at) in enumerate(places):
                acc[0, at] += band[t * BR : (t + 1) * BR] * w
                acc[1, at] += band[KR + t * BR : KR + (t + 1) * BR] * w
    saves = []
    for chunk in range(4):
        rows = slice(chunk * 64, chunk * 64 + 64)
        sre = mine[0, rows].astype(F32)
        sim = mine[1, rows].astype(F32)
        are, aim = acc[0, rows], acc[1, rows]
        out_re = (sre * are + sim * aim).reshape(8, ROWS, NX)
        out_im = (sre * aim - sim * are).reshape(8, ROWS, NX)
        here = slice(chunk * 8, chunk * 8 + 8)
        out_ref[here] = jnp.concatenate([out_re, out_im], axis=1).astype(BF16)
        saves.append(pltpu.make_async_copy(out_ref.at[here], out.at[here], out_sem.at[chunk]))
        saves[-1].start()
    for save in saves:
        save.wait()


def applied_kernel(parts_ref, r_ref, p_ref, low_ref, high_ref, applied_ref, sums_ref):
    totals = [jnp.zeros((ROWS, NX), F32) for _ in range(4)]
    for q in range(2):
        total = jnp.zeros((2 * ROWS, NX), F32)
        for pair in range(2):
            for xc in range(8):
                total = total + parts_ref[(pair * 2 + q) * 8 + xc].astype(F32)
        for c in range(2):
            p = p_ref[0, q, c]
            r = r_ref[0, q, c]
            smooth = 2.0 * p - low_ref[0, q, c].astype(F32) - high_ref[0, q, c].astype(F32)
            applied = total[c * ROWS : (c + 1) * ROWS] + reg_weight * smooth + shift_weight * p
            applied_ref[0, q, c] = applied
            for i, term in enumerate((r * r, p * applied, r * applied, applied * applied)):
                totals[i] = totals[i] + term
    lane = lax.broadcasted_iota(jnp.int32, (8, 128), 1)
    line = jnp.zeros((8, 128), F32)
    for i in range(4):
        whole = jnp.sum(jnp.sum(totals[i], axis=0, keepdims=True), axis=1, keepdims=True)
        line = jnp.where(lane == i, whole, line)
    sums_ref[...] = jnp.broadcast_to(line[:1, :8], (DEVICES, 8))


def update_kernel(sums_ref, x_ref, r_ref, p_ref, applied_ref, x_out, r_out, p_out):
    sums = jnp.sum(sums_ref[...], axis=0, keepdims=True)
    rr, pa, ra, aa = (sums[:, i : i + 1] for i in range(4))
    alpha = rr / (pa + epsilon)
    rnew = rr - 2.0 * alpha * ra + alpha * alpha * aa
    beta = rnew / (rr + epsilon)
    alpha = jnp.broadcast_to(alpha, (ROWS, NX))
    beta = jnp.broadcast_to(beta, (ROWS, NX))
    for q in range(2):
        for c in range(2):
            p = p_ref[0, q, c]
            r = r_ref[0, q, c] - alpha * applied_ref[0, q, c]
            x_out[0, q, c] = x_ref[0, q, c] + alpha * p
            r_out[0, q, c] = r
            p_out[0, q, c] = r + beta * p


VM = pl.BlockSpec(memory_space=pltpu.VMEM)
HB = pl.BlockSpec(memory_space=pltpu.HBM)


def hbm(array):
    return pltpu.with_memory_space_constraint(array, pltpu.HBM)


def local(x_in, r_in, p_in, sens, seg_weights, seg_freq, band_ids, seg_count, k_bands):
    half_shape = jax.ShapeDtypeStruct((SEGS_DEV, HALF, BR, NX), BF16)
    send, same, other = pl.pallas_call(
        prep_kernel,
        in_specs=[VM, VM],
        out_specs=[VM, VM, VM],
        out_shape=[jax.ShapeDtypeStruct((GROUP, 2 * ROWS, NX), jnp.int16), half_shape, half_shape],
        compiler_params=pltpu.CompilerParams(vmem_limit_bytes=4 << 20),
        name="prep",
    )(hbm(p_in), hbm(seg_weights))
    halves = [
        lax.ppermute(same if k == 2 else other, "segments", [(i, (i + k) % 4) for i in range(4)])
        for k in (1, 2, 3)
    ]
    whole = lax.all_to_all(send, SPACE, 0, 0, tiled=True)
    halo = p_in.astype(BF16)
    low = lax.ppermute(halo, "frames", [(i, (i + 1) % 8) for i in range(8)])
    high = lax.ppermute(halo, "frames", [(i, (i + 7) % 8) for i in range(8)])
    bands = hbm(band_ids.T)
    g, ft, gx, elapsed, quarter = pl.pallas_call(
        tables_kernel,
        in_specs=[HB] * 3,
        out_specs=[VM] * 5,
        out_shape=[
            jax.ShapeDtypeStruct((NSEG, 2 * KR, 2 * KR), BF16),
            jax.ShapeDtypeStruct((2, NY, 2 * KR), BF16),
            jax.ShapeDtypeStruct((2, NX, NX), BF16),
            jax.ShapeDtypeStruct((KR, NX), F32),
            jax.ShapeDtypeStruct((NSEG, 1, NX), F32),
        ],
        scratch_shapes=[
            pltpu.VMEM((2, 2 * KR, NY), BF16),
            pltpu.SMEM((OT, NSEG), jnp.int32),
            pltpu.SMEM((1, KR // KB), jnp.int32),
            pltpu.SMEM((NSEG,), F32),
            pltpu.SemaphoreType.DMA((3,)),
        ],
        compiler_params=pltpu.CompilerParams(vmem_limit_bytes=32 << 20),
        cost_estimate=pl.CostEstimate(flops=1_000_000_000, bytes_accessed=2 << 20, transcendentals=0),
        name="tables",
    )(bands, hbm(k_bands), hbm(seg_freq))
    turn = pl.pallas_call(
        turns_kernel,
        in_specs=[VM, VM] + [pl.BlockSpec(memory_space=pl.ANY)] * 3,
        out_specs=HB,
        out_shape=pltpu.HBM((NSEG, 2, KR, NX), F32),
        scratch_shapes=[pltpu.VMEM((NSEG, 2, KR, NX), F32), pltpu.SemaphoreType.DMA((NSEG,))],
        compiler_params=pltpu.CompilerParams(vmem_limit_bytes=32 << 20),
        cost_estimate=pl.CostEstimate(flops=40_000_000_000, bytes_accessed=3 << 20, transcendentals=0),
        name="turns",
    )(elapsed, quarter, *halves)
    others = [lax.ppermute(half, "coils", [(i, i ^ 1) for i in range(8)]) for half in halves]
    parts = pl.pallas_call(
        normal_kernel,
        in_specs=[HB] * 2 + [VM] * 10 + [HB] * 3,
        out_specs=HB,
        out_shape=pltpu.HBM((GROUP, 2 * ROWS, NX), BF16),
        scratch_shapes=[
            pltpu.VMEM((2, NY, NX), F32),
            pltpu.VMEM((NSEG, 2 * KR, NX), BF16),
            pltpu.VMEM((NSEG * KR, 2 * NX), BF16),
            pltpu.VMEM((2, KR, NX), F32),
            pltpu.VMEM((2, NY, NX), F32),
            pltpu.VMEM((2, NY, NX), BF16),
            pltpu.VMEM((2, SEGS_DEV, HALF, BR, NX), BF16),
            pltpu.VMEM((2, 2 * NX, 2 * NX), BF16),
            pltpu.VMEM((NSEG, 2, KR, NX), F32),
            pltpu.VMEM((GROUP, 2 * ROWS, NX), BF16),
            pltpu.SMEM((OT, NSEG), jnp.int32),
            pltpu.SMEM((NSEG,), jnp.int32),
            pltpu.SemaphoreType.DMA((6,)),
            pltpu.SemaphoreType.DMA((4,)),
        ],
        compiler_params=pltpu.CompilerParams(vmem_limit_bytes=32 << 20),
        cost_estimate=pl.CostEstimate(flops=2_400_000_000, bytes_accessed=8 << 20, transcendentals=0),
        name="normal",
    )(
        bands, hbm(seg_count), whole, g, ft, gx,
        halves[0], others[0], halves[1], others[1], halves[2], others[2], hbm(sens), hbm(seg_weights), hbm(turn),
    )
    parts = lax.all_to_all(parts, SPACE, 0, 0, tiled=True)
    share = jax.ShapeDtypeStruct(p_in.shape, F32)
    applied, sums = pl.pallas_call(
        applied_kernel,
        in_specs=[VM] * 5,
        out_specs=[VM, VM],
        out_shape=[share, jax.ShapeDtypeStruct((DEVICES, 8), F32)],
        compiler_params=pltpu.CompilerParams(vmem_limit_bytes=4 << 20),
        name="applied",
    )(parts, r_in, p_in, low, high)
    sums = lax.all_to_all(sums, ("frames", "segments", "coils"), 0, 0, tiled=True)
    return tuple(
        pl.pallas_call(
            update_kernel,
            in_specs=[VM] * 5,
            out_specs=[VM] * 3,
            out_shape=[share] * 3,
            compiler_params=pltpu.CompilerParams(vmem_limit_bytes=4 << 20),
            name="update",
        )(sums, x_in, r_in, p_in, applied)
    )


def solution(mesh):
    image = P("frames", None, None, ("segments", "coils"), None)
    in_specs = (
        image,
        image,
        image,
        P("coils", None, None, None, None),
        P("segments", None, None, None, None),
        P(),
        P(),
        P(),
        P("frames", None),
    )
    return jax.shard_map(local, mesh=mesh, in_specs=in_specs, out_specs=(image,) * 3, check_vma=False)
```

```python
import math

import jax
import jax.numpy as jnp
from jax import lax
from jax.experimental import pallas as pl
from jax.experimental.pallas import tpu as pltpu
from jax.sharding import PartitionSpec as P

BR = 16
KB = 8
NX = 256
NY = 256
OT = 8
NSEG = 12
KR = 128
SEGS_DEV = 3
YDEV = 4
GROUP = 32
ROWS = 8
HALF = OT // 2
DEVICES = 256
CODE = 32767.0 / 6.0

reg_weight = 0.5
shift_weight = 0.1
epsilon = 1e-06

F32 = jnp.float32
BF16 = jnp.bfloat16
SPACE = ("segments", "coils")


def sin_cos(quarter):
    sq = quarter * quarter
    s = F32(1.0 / math.factorial(9))
    for n in (7, 5, 3, 1):
        s = s * sq + F32((-1.0) ** (n // 2) / math.factorial(n))
    s = s * quarter
    c = F32(-1.0 / math.factorial(10))
    for n in (8, 6, 4, 2, 0):
        c = c * sq + F32((-1.0) ** (n // 2) / math.factorial(n))
    twice = s + s
    s, c = twice * c, 1.0 - twice * s
    twice = s + s
    return twice * c, 1.0 - twice * s


def unit_parts(products):
    n = ((products + 128) & 255) - 128
    s, c = sin_cos(n.astype(F32) * F32(0.5 * math.pi / 256))
    return c * F32(1.0 / 16.0), s * F32(-1.0 / 16.0)


def segment_of(slot):
    y = lax.axis_index("segments")
    return lax.rem(y - slot // SEGS_DEV + YDEV, YDEV) * SEGS_DEV + slot % SEGS_DEV


def block_of(place):
    core = lax.rem(lax.axis_index("coils"), 2)
    return lax.rem(core * HALF + place, OT)


def spread(values, index, width):
    out = jnp.zeros_like(index)
    for j, value in enumerate(values):
        out = jnp.where(index // width == j, value * width + index % width, out)
    return out


def prep_kernel(p_ref, w_ref, send_ref, same_ref, other_ref):
    plane = lax.rem(lax.axis_index("segments"), 2)
    core = lax.rem(lax.axis_index("coils"), 2)
    for i in range(SEGS_DEV):
        for t in range(HALF):
            same_ref[i, t] = w_ref[i, core * HALF + t, plane]
            other_ref[i, t] = w_ref[i, core * HALF + t, 1 - plane]
    for q in range(2):
        both = jnp.concatenate([p_ref[0, q, 0], p_ref[0, q, 1]], axis=0)
        code = jnp.floor(both * F32(CODE) + 0.5).astype(jnp.int32).astype(jnp.int16)
        for pair in range(2):
            for xc in range(8):
                send_ref[(pair * 2 + q) * 8 + xc] = code


def turns_kernel(elapsed_ref, freq_ref, h1, h2, h3, turn_out, turn, turn_sem):
    saves = [pltpu.make_async_copy(turn.at[slot], turn_out.at[slot], turn_sem.at[slot]) for slot in range(NSEG)]
    for slot in range(NSEG):
        turn[slot, 1], turn[slot, 0] = sin_cos(freq_ref[slot] * elapsed_ref[...])
        saves[slot].start()
    for save in saves:
        save.wait()


def tables_kernel(
    bands_in, kb_in, freq_in, sens_in, g_ref, ft, gx_ref, elapsed_ref, quarter_ref, mine_ref, e, bands_ref, kb_ref, freq_ref, sem
):
    loads = [
        pltpu.make_async_copy(source, target, sem.at[i])
        for i, (source, target) in enumerate([(bands_in, bands_ref), (kb_in, kb_ref), (freq_in, freq_ref)])
    ]
    y = lax.axis_index("segments")
    fetch = pltpu.make_async_copy(sens_in.at[y // 2, lax.rem(y, 2)], mine_ref, sem.at[3])
    for load in loads:
        load.start()
    fetch.start()
    rows = lax.broadcasted_iota(jnp.int32, (NX, NX), 0)
    cols = lax.broadcasted_iota(jnp.int32, (NX, NX), 1)
    re, im = unit_parts(rows * cols)
    gx_ref[0] = re.astype(BF16)
    gx_ref[1] = im.astype(BF16)
    for load in loads:
        load.wait()
    for slot in range(NSEG):
        quarter_ref[slot] = jnp.broadcast_to(freq_ref[segment_of(slot)] * F32(0.25), (1, NX))
    kbs = [kb_ref[0, j] for j in range(KR // KB)]
    ky_col = spread(kbs, lax.broadcasted_iota(jnp.int32, (KR, KR), 0), KB)
    ky_wide = jnp.concatenate([ky_col, ky_col], axis=1)
    cy = (((ky_wide + 128) & 255) - 128).astype(F32) * F32(1.0 / 128.0)
    cx_index = lax.broadcasted_iota(jnp.int32, (KR, NX), 1)
    cx = (((cx_index + 128) & 255) - 128).astype(F32) * F32(1.0 / 128.0)
    elapsed_ref[...] = jnp.sqrt(cy * cy + cx * cx)
    ky_row = spread(kbs, lax.broadcasted_iota(jnp.int32, (8, KR), 1), KB)[:1]
    re, im = unit_parts(lax.broadcasted_iota(jnp.int32, (NY, KR), 0) * ky_row)
    ft[0, :, :KR] = re.astype(BF16)
    ft[0, :, KR:] = im.astype(BF16)
    ft[1, :, :KR] = (-im).astype(BF16)
    ft[1, :, KR:] = re.astype(BF16)
    re, im = unit_parts(ky_wide * lax.broadcasted_iota(jnp.int32, (KR, NY), 1))
    e[0, :KR] = re.astype(BF16)
    e[0, KR:] = im.astype(BF16)
    e[1, :KR] = (-im).astype(BF16)
    e[1, KR:] = re.astype(BF16)
    image_row = lax.broadcasted_iota(jnp.int32, (NY, KR), 0)
    for slot in range(NSEG):
        seg = segment_of(slot)
        bands = [bands_ref[block_of(t), seg] for t in range(OT)]
        yr_row = spread(bands, lax.broadcasted_iota(jnp.int32, (8, KR), 1), BR)[:1]
        pick = jnp.where(image_row == yr_row, F32(1), F32(0)).astype(BF16)
        g_ref[slot, :, :KR] = mm(e[0], pick).astype(BF16)
        g_ref[slot, :, KR:] = mm(e[1], pick).astype(BF16)
    fetch.wait()


def mm(a, b):
    return jnp.dot(a, b, preferred_element_type=F32)


def normal_kernel(
    bands_in, count_in, p_ref, g, ft, gx_ref, h1, o1, h2, o2, h3, o3, mine, w_in, turn_in, out,
    coil, blk, first, ks, acc, near, gx, turn, out_ref, bands_ref, count_ref, sem, out_sem,
):
    y = lax.axis_index("segments")
    plane = lax.rem(y, 2)
    core = lax.rem(lax.axis_index("coils"), 2)
    loads = [
        pltpu.make_async_copy(source, target, sem.at[i])
        for i, (source, target) in enumerate(
            [
                (w_in.at[:, pl.ds(core * HALF, HALF), plane], near.at[0]),
                (w_in.at[:, pl.ds((1 - core) * HALF, HALF), plane], near.at[1]),
                (bands_in, bands_ref),
                (count_in, count_ref),
                *((turn_in.at[i : i + 2], turn.at[i : i + 2]) for i in range(0, NSEG, 2)),
            ]
        )
    ]
    for load in loads:
        load.start()
    halves = ((near.at[0], near.at[1]), (h1, o1), (h2, o2), (h3, o3))
    gre, gim = gx_ref[0], gx_ref[1]
    for i, sign in enumerate((1, -1)):
        gx[i, :NX, :NX] = gre
        gx[i, :NX, NX:] = sign * gim
        gx[i, NX:, :NX] = -sign * gim
        gx[i, NX:, NX:] = gre

    def weight(slot, t):
        seg = segment_of(slot)
        j = block_of(t)
        live = (j < count_ref[seg]).astype(F32)
        w = halves[slot // SEGS_DEV][t // HALF][slot % SEGS_DEV, t % HALF]
        at = pl.ds(pl.multiple_of(bands_ref[j, seg] * BR, BR), BR)
        return w.astype(F32) * live, at

    acc[...] = jnp.zeros_like(acc)
    for chunk in range(4):
        rows = slice(chunk * 64, chunk * 64 + 64)
        p = p_ref[chunk * 8 : chunk * 8 + 8].astype(jnp.int32).astype(F32) * F32(1.0 / CODE)
        pre = p[:, :ROWS].reshape(64, NX)
        pim = p[:, ROWS:].reshape(64, NX)
        sre = mine[0, rows].astype(F32)
        sim = mine[1, rows].astype(F32)
        coil[0, rows] = sre * pre - sim * pim
        coil[1, rows] = sre * pim + sim * pre
    for load in loads[:4]:
        load.wait()
    for slot in range(NSEG):
        for t in range(OT):
            w, at = weight(slot, t)
            blk[slot, t * BR : (t + 1) * BR] = (coil[0, at] * w).astype(BF16)
            blk[slot, KR + t * BR : KR + (t + 1) * BR] = (coil[1, at] * w).astype(BF16)
        got = mm(g[slot], blk[slot]).astype(BF16)
        first[slot * KR : (slot + 1) * KR, :NX] = got[:KR]
        first[slot * KR : (slot + 1) * KR, NX:] = got[KR:]
    for load in loads[4:]:
        load.wait()
    for pair in range(NSEG // 2):
        spec = mm(first[pair * 2 * KR : (pair + 1) * 2 * KR], gx[0])
        tre, tim = 0.0, 0.0
        for half in range(2):
            re, im = spec[half * KR : (half + 1) * KR, :NX], spec[half * KR : (half + 1) * KR, NX:]
            c, s = turn[pair * 2 + half, 0], turn[pair * 2 + half, 1]
            tre = tre + (re * c + im * s)
            tim = tim + (im * c - re * s)
        ks[0] = tre if pair == 0 else ks[0] + tre
        ks[1] = tim if pair == 0 else ks[1] + tim
    def demod(pair):
        re, im = ks[0], ks[1]
        for half in range(2):
            c, s = turn[pair * 2 + half, 0], turn[pair * 2 + half, 1]
            here = slice((pair * 2 + half) * KR, (pair * 2 + half + 1) * KR)
            first[here, :NX] = (re * c - im * s).astype(BF16)
            first[here, NX:] = (im * c + re * s).astype(BF16)

    def back_mm(pair):
        back = mm(first[pair * 2 * KR : (pair + 1) * 2 * KR], gx[1]).astype(BF16)
        for half in range(2):
            blk[pair * 2 + half, :KR] = back[half * KR : (half + 1) * KR, :NX]
            blk[pair * 2 + half, KR:] = back[half * KR : (half + 1) * KR, NX:]

    def gather(pair):
        for half in range(2):
            slot = pair * 2 + half
            places = [weight(slot, t) for t in range(OT)]
            rows = jnp.concatenate([ft[c, at] for c in range(2) for _, at in places], axis=0)
            band = mm(rows, blk[slot])
            for t, (w, at) in enumerate(places):
                acc[0, at] += band[t * BR : (t + 1) * BR] * w
                acc[1, at] += band[KR + t * BR : KR + (t + 1) * BR] * w

    pairs = NSEG // 2
    demod(0)
    for pair in range(pairs + 1):
        if pair < pairs:
            back_mm(pair)
        if pair + 1 < pairs:
            demod(pair + 1)
        if pair:
            gather(pair - 1)
    saves = []
    for chunk in range(4):
        rows = slice(chunk * 64, chunk * 64 + 64)
        sre = mine[0, rows].astype(F32)
        sim = mine[1, rows].astype(F32)
        are, aim = acc[0, rows], acc[1, rows]
        out_re = (sre * are + sim * aim).reshape(8, ROWS, NX)
        out_im = (sre * aim - sim * are).reshape(8, ROWS, NX)
        here = slice(chunk * 8, chunk * 8 + 8)
        out_ref[here] = jnp.concatenate([out_re, out_im], axis=1).astype(BF16)
        saves.append(pltpu.make_async_copy(out_ref.at[here], out.at[here], out_sem.at[chunk]))
        saves[-1].start()
    for save in saves:
        save.wait()


def applied_kernel(parts_ref, r_ref, p_ref, low_ref, high_ref, applied_ref, sums_ref):
    totals = [jnp.zeros((ROWS, NX), F32) for _ in range(4)]
    for q in range(2):
        total = jnp.zeros((2 * ROWS, NX), F32)
        for pair in range(2):
            for xc in range(8):
                total = total + parts_ref[(pair * 2 + q) * 8 + xc].astype(F32)
        for c in range(2):
            p = p_ref[0, q, c]
            r = r_ref[0, q, c]
            smooth = 2.0 * p - low_ref[0, q, c].astype(F32) - high_ref[0, q, c].astype(F32)
            applied = total[c * ROWS : (c + 1) * ROWS] + reg_weight * smooth + shift_weight * p
            applied_ref[0, q, c] = applied
            for i, term in enumerate((r * r, p * applied, r * applied, applied * applied)):
                totals[i] = totals[i] + term
    lane = lax.broadcasted_iota(jnp.int32, (8, 128), 1)
    line = jnp.zeros((8, 128), F32)
    for i in range(4):
        whole = jnp.sum(jnp.sum(totals[i], axis=0, keepdims=True), axis=1, keepdims=True)
        line = jnp.where(lane == i, whole, line)
    sums_ref[...] = jnp.broadcast_to(line[:1, :8], (DEVICES, 8))


def update_kernel(sums_ref, x_ref, r_ref, p_ref, applied_ref, x_out, r_out, p_out):
    sums = jnp.sum(sums_ref[...], axis=0, keepdims=True)
    rr, pa, ra, aa = (sums[:, i : i + 1] for i in range(4))
    alpha = rr / (pa + epsilon)
    rnew = rr - 2.0 * alpha * ra + alpha * alpha * aa
    beta = rnew / (rr + epsilon)
    alpha = jnp.broadcast_to(alpha, (ROWS, NX))
    beta = jnp.broadcast_to(beta, (ROWS, NX))
    for q in range(2):
        for c in range(2):
            p = p_ref[0, q, c]
            r = r_ref[0, q, c] - alpha * applied_ref[0, q, c]
            x_out[0, q, c] = x_ref[0, q, c] + alpha * p
            r_out[0, q, c] = r
            p_out[0, q, c] = r + beta * p


VM = pl.BlockSpec(memory_space=pltpu.VMEM)
HB = pl.BlockSpec(memory_space=pltpu.HBM)


def hbm(array):
    return pltpu.with_memory_space_constraint(array, pltpu.HBM)


def local(x_in, r_in, p_in, sens, seg_weights, seg_freq, band_ids, seg_count, k_bands):
    half_shape = jax.ShapeDtypeStruct((SEGS_DEV, HALF, BR, NX), BF16)
    send, same, other = pl.pallas_call(
        prep_kernel,
        in_specs=[VM, VM],
        out_specs=[VM, VM, VM],
        out_shape=[jax.ShapeDtypeStruct((GROUP, 2 * ROWS, NX), jnp.int16), half_shape, half_shape],
        compiler_params=pltpu.CompilerParams(vmem_limit_bytes=4 << 20),
        name="prep",
    )(hbm(p_in), hbm(seg_weights))
    halves = [
        lax.ppermute(same if k == 2 else other, "segments", [(i, (i + k) % 4) for i in range(4)])
        for k in (1, 2, 3)
    ]
    whole = lax.all_to_all(send, SPACE, 0, 0, tiled=True)
    halo = p_in.astype(BF16)
    low = lax.ppermute(halo, "frames", [(i, (i + 1) % 8) for i in range(8)])
    high = lax.ppermute(halo, "frames", [(i, (i + 7) % 8) for i in range(8)])
    bands = hbm(band_ids.T)
    g, ft, gx, elapsed, quarter, mine = pl.pallas_call(
        tables_kernel,
        in_specs=[HB] * 4,
        out_specs=[VM] * 6,
        out_shape=[
            jax.ShapeDtypeStruct((NSEG, 2 * KR, 2 * KR), BF16),
            jax.ShapeDtypeStruct((2, NY, 2 * KR), BF16),
            jax.ShapeDtypeStruct((2, NX, NX), BF16),
            jax.ShapeDtypeStruct((KR, NX), F32),
            jax.ShapeDtypeStruct((NSEG, 1, NX), F32),
            jax.ShapeDtypeStruct((2, NY, NX), BF16),
        ],
        scratch_shapes=[
            pltpu.VMEM((2, 2 * KR, NY), BF16),
            pltpu.SMEM((OT, NSEG), jnp.int32),
            pltpu.SMEM((1, KR // KB), jnp.int32),
            pltpu.SMEM((NSEG,), F32),
            pltpu.SemaphoreType.DMA((4,)),
        ],
        compiler_params=pltpu.CompilerParams(vmem_limit_bytes=32 << 20),
        cost_estimate=pl.CostEstimate(flops=1_000_000_000, bytes_accessed=2 << 20, transcendentals=0),
        name="tables",
    )(bands, hbm(k_bands), hbm(seg_freq), hbm(sens))
    turn = pl.pallas_call(
        turns_kernel,
        in_specs=[VM, VM] + [pl.BlockSpec(memory_space=pl.ANY)] * 3,
        out_specs=HB,
        out_shape=pltpu.HBM((NSEG, 2, KR, NX), F32),
        scratch_shapes=[pltpu.VMEM((NSEG, 2, KR, NX), F32), pltpu.SemaphoreType.DMA((NSEG,))],
        compiler_params=pltpu.CompilerParams(vmem_limit_bytes=32 << 20),
        cost_estimate=pl.CostEstimate(flops=40_000_000_000, bytes_accessed=3 << 20, transcendentals=0),
        name="turns",
    )(elapsed, quarter, *halves)
    others = [lax.ppermute(half, "coils", [(i, i ^ 1) for i in range(8)]) for half in halves]
    parts = pl.pallas_call(
        normal_kernel,
        in_specs=[HB] * 2 + [VM] * 11 + [HB] * 2,
        out_specs=HB,
        out_shape=pltpu.HBM((GROUP, 2 * ROWS, NX), BF16),
        scratch_shapes=[
            pltpu.VMEM((2, NY, NX), F32),
            pltpu.VMEM((NSEG, 2 * KR, NX), BF16),
            pltpu.VMEM((NSEG * KR, 2 * NX), BF16),
            pltpu.VMEM((2, KR, NX), F32),
            pltpu.VMEM((2, NY, NX), F32),
            pltpu.VMEM((2, SEGS_DEV, HALF, BR, NX), BF16),
            pltpu.VMEM((2, 2 * NX, 2 * NX), BF16),
            pltpu.VMEM((NSEG, 2, KR, NX), F32),
            pltpu.VMEM((GROUP, 2 * ROWS, NX), BF16),
            pltpu.SMEM((OT, NSEG), jnp.int32),
            pltpu.SMEM((NSEG,), jnp.int32),
            pltpu.SemaphoreType.DMA((10,)),
            pltpu.SemaphoreType.DMA((4,)),
        ],
        compiler_params=pltpu.CompilerParams(vmem_limit_bytes=32 << 20),
        cost_estimate=pl.CostEstimate(flops=2_400_000_000, bytes_accessed=8 << 20, transcendentals=0),
        name="normal",
    )(
        bands, hbm(seg_count), whole, g, ft, gx,
        halves[0], others[0], halves[1], others[1], halves[2], others[2], mine, hbm(seg_weights), hbm(turn),
    )
    parts = lax.all_to_all(parts, SPACE, 0, 0, tiled=True)
    share = jax.ShapeDtypeStruct(p_in.shape, F32)
    applied, sums = pl.pallas_call(
        applied_kernel,
        in_specs=[VM] * 5,
        out_specs=[VM, VM],
        out_shape=[share, jax.ShapeDtypeStruct((DEVICES, 8), F32)],
        compiler_params=pltpu.CompilerParams(vmem_limit_bytes=4 << 20),
        name="applied",
    )(parts, r_in, p_in, low, high)
    sums = lax.all_to_all(sums, ("frames", "segments", "coils"), 0, 0, tiled=True)
    return tuple(
        pl.pallas_call(
            update_kernel,
            in_specs=[VM] * 5,
            out_specs=[VM] * 3,
            out_shape=[share] * 3,
            compiler_params=pltpu.CompilerParams(vmem_limit_bytes=4 << 20),
            name="update",
        )(sums, x_in, r_in, p_in, applied)
    )


def solution(mesh):
    image = P("frames", None, None, ("segments", "coils"), None)
    in_specs = (
        image,
        image,
        image,
        P("coils", None, None, None, None),
        P("segments", None, None, None, None),
        P(),
        P(),
        P(),
        P("frames", None),
    )
    return jax.shard_map(local, mesh=mesh, in_specs=in_specs, out_specs=(image,) * 3, check_vma=False)
```

```python
import math

import jax
import jax.numpy as jnp
from jax import lax
from jax.experimental import pallas as pl
from jax.experimental.pallas import tpu as pltpu
from jax.sharding import PartitionSpec as P

BR = 16
KB = 8
NX = 256
NY = 256
OT = 8
NSEG = 12
KR = 128
SEGS_DEV = 3
YDEV = 4
GROUP = 32
ROWS = 8
HALF = OT // 2
DEVICES = 256
CODE = 32767.0 / 6.0

reg_weight = 0.5
shift_weight = 0.1
epsilon = 1e-06

F32 = jnp.float32
BF16 = jnp.bfloat16
SPACE = ("segments", "coils")


def sin_cos(quarter):
    sq = quarter * quarter
    s = F32(1.0 / math.factorial(9))
    for n in (7, 5, 3, 1):
        s = s * sq + F32((-1.0) ** (n // 2) / math.factorial(n))
    s = s * quarter
    c = F32(-1.0 / math.factorial(10))
    for n in (8, 6, 4, 2, 0):
        c = c * sq + F32((-1.0) ** (n // 2) / math.factorial(n))
    twice = s + s
    s, c = twice * c, 1.0 - twice * s
    twice = s + s
    return twice * c, 1.0 - twice * s


def unit_parts(products):
    n = ((products + 128) & 255) - 128
    s, c = sin_cos(n.astype(F32) * F32(0.5 * math.pi / 256))
    return c * F32(1.0 / 16.0), s * F32(-1.0 / 16.0)


def segment_of(slot):
    y = lax.axis_index("segments")
    return lax.rem(y - slot // SEGS_DEV + YDEV, YDEV) * SEGS_DEV + slot % SEGS_DEV


def block_of(place):
    core = lax.rem(lax.axis_index("coils"), 2)
    return lax.rem(core * HALF + place, OT)


def spread(values, index, width):
    out = jnp.zeros_like(index)
    for j, value in enumerate(values):
        out = jnp.where(index // width == j, value * width + index % width, out)
    return out


def prep_kernel(p_in, w_in, send_out, same_ref, other_ref, p_ref, w_ref, code, sem, send_sem):
    plane = lax.rem(lax.axis_index("segments"), 2)
    core = lax.rem(lax.axis_index("coils"), 2)
    load_p = pltpu.make_async_copy(p_in, p_ref, sem.at[0])
    load_w = pltpu.make_async_copy(w_in.at[:, pl.ds(core * HALF, HALF)], w_ref, sem.at[1])
    load_p.start()
    load_w.start()
    load_p.wait()
    saves = []
    for q in range(2):
        both = jnp.concatenate([p_ref[0, q, 0], p_ref[0, q, 1]], axis=0)
        value = jnp.floor(both * F32(CODE) + 0.5).astype(jnp.int32).astype(jnp.int16)
        for xc in range(8):
            code[q, xc] = value
        for pair in range(2):
            target = send_out.at[pl.ds((pair * 2 + q) * 8, 8)]
            saves.append(pltpu.make_async_copy(code.at[q], target, send_sem.at[pair * 2 + q]))
            saves[-1].start()
    load_w.wait()
    for i in range(SEGS_DEV):
        for t in range(HALF):
            same_ref[i, t] = w_ref[i, t, plane]
            other_ref[i, t] = w_ref[i, t, 1 - plane]
    for save in saves:
        save.wait()


def turns_kernel(elapsed_ref, freq_ref, h1, h2, h3, turn_out, turn, turn_sem):
    saves = [pltpu.make_async_copy(turn.at[slot], turn_out.at[slot], turn_sem.at[slot]) for slot in range(NSEG)]
    for slot in range(NSEG):
        turn[slot, 1], turn[slot, 0] = sin_cos(freq_ref[slot] * elapsed_ref[...])
        saves[slot].start()
    for save in saves:
        save.wait()


def tables_kernel(
    bands_in, kb_in, freq_in, sens_in, g_ref, ft, gx_ref, elapsed_ref, quarter_ref, mine_ref, e, bands_ref, kb_ref, freq_ref, sem
):
    loads = [
        pltpu.make_async_copy(source, target, sem.at[i])
        for i, (source, target) in enumerate([(bands_in, bands_ref), (kb_in, kb_ref), (freq_in, freq_ref)])
    ]
    y = lax.axis_index("segments")
    fetch = pltpu.make_async_copy(sens_in.at[y // 2, lax.rem(y, 2)], mine_ref, sem.at[3])
    for load in loads:
        load.start()
    fetch.start()
    rows = lax.broadcasted_iota(jnp.int32, (NX, NX), 0)
    cols = lax.broadcasted_iota(jnp.int32, (NX, NX), 1)
    re, im = unit_parts(rows * cols)
    gx_ref[0] = re.astype(BF16)
    gx_ref[1] = im.astype(BF16)
    for load in loads:
        load.wait()
    for slot in range(NSEG):
        quarter_ref[slot] = jnp.broadcast_to(freq_ref[segment_of(slot)] * F32(0.25), (1, NX))
    kbs = [kb_ref[0, j] for j in range(KR // KB)]
    ky_col = spread(kbs, lax.broadcasted_iota(jnp.int32, (KR, KR), 0), KB)
    ky_wide = jnp.concatenate([ky_col, ky_col], axis=1)
    cy = (((ky_wide + 128) & 255) - 128).astype(F32) * F32(1.0 / 128.0)
    cx_index = lax.broadcasted_iota(jnp.int32, (KR, NX), 1)
    cx = (((cx_index + 128) & 255) - 128).astype(F32) * F32(1.0 / 128.0)
    elapsed_ref[...] = jnp.sqrt(cy * cy + cx * cx)
    ky_row = spread(kbs, lax.broadcasted_iota(jnp.int32, (8, KR), 1), KB)[:1]
    re, im = unit_parts(lax.broadcasted_iota(jnp.int32, (NY, KR), 0) * ky_row)
    ft[0, :, :KR] = re.astype(BF16)
    ft[0, :, KR:] = im.astype(BF16)
    ft[1, :, :KR] = (-im).astype(BF16)
    ft[1, :, KR:] = re.astype(BF16)
    re, im = unit_parts(ky_wide * lax.broadcasted_iota(jnp.int32, (KR, NY), 1))
    e[0, :KR] = re.astype(BF16)
    e[0, KR:] = im.astype(BF16)
    e[1, :KR] = (-im).astype(BF16)
    e[1, KR:] = re.astype(BF16)
    image_row = lax.broadcasted_iota(jnp.int32, (NY, KR), 0)
    for slot in range(NSEG):
        seg = segment_of(slot)
        bands = [bands_ref[block_of(t), seg] for t in range(OT)]
        yr_row = spread(bands, lax.broadcasted_iota(jnp.int32, (8, KR), 1), BR)[:1]
        pick = jnp.where(image_row == yr_row, F32(1), F32(0)).astype(BF16)
        g_ref[slot, :, :KR] = mm(e[0], pick).astype(BF16)
        g_ref[slot, :, KR:] = mm(e[1], pick).astype(BF16)
    fetch.wait()


def mm(a, b):
    return jnp.dot(a, b, preferred_element_type=F32)


def normal_kernel(
    bands_in, count_in, p_ref, g, ft, gx_ref, h1, o1, h2, o2, h3, o3, mine, w_in, turn_in, out,
    coil, blk, first, ks, acc, near, gx, turn, out_ref, bands_ref, count_ref, sem, out_sem,
):
    y = lax.axis_index("segments")
    plane = lax.rem(y, 2)
    core = lax.rem(lax.axis_index("coils"), 2)
    loads = [
        pltpu.make_async_copy(source, target, sem.at[i])
        for i, (source, target) in enumerate(
            [
                (w_in.at[:, pl.ds(core * HALF, HALF), plane], near.at[0]),
                (w_in.at[:, pl.ds((1 - core) * HALF, HALF), plane], near.at[1]),
                (bands_in, bands_ref),
                (count_in, count_ref),
                *((turn_in.at[i : i + 2], turn.at[i : i + 2]) for i in range(0, NSEG, 2)),
            ]
        )
    ]
    for load in loads:
        load.start()
    halves = ((near.at[0], near.at[1]), (h1, o1), (h2, o2), (h3, o3))
    gre, gim = gx_ref[0], gx_ref[1]
    for i, sign in enumerate((1, -1)):
        gx[i, :NX, :NX] = gre
        gx[i, :NX, NX:] = sign * gim
        gx[i, NX:, :NX] = -sign * gim
        gx[i, NX:, NX:] = gre

    def weight(slot, t):
        seg = segment_of(slot)
        j = block_of(t)
        live = (j < count_ref[seg]).astype(F32)
        w = halves[slot // SEGS_DEV][t // HALF][slot % SEGS_DEV, t % HALF]
        at = pl.ds(pl.multiple_of(bands_ref[j, seg] * BR, BR), BR)
        return w.astype(F32) * live, at

    acc[...] = jnp.zeros_like(acc)
    for chunk in range(4):
        rows = slice(chunk * 64, chunk * 64 + 64)
        p = p_ref[chunk * 8 : chunk * 8 + 8].astype(jnp.int32).astype(F32) * F32(1.0 / CODE)
        pre = p[:, :ROWS].reshape(64, NX)
        pim = p[:, ROWS:].reshape(64, NX)
        sre = mine[0, rows].astype(F32)
        sim = mine[1, rows].astype(F32)
        coil[0, rows] = sre * pre - sim * pim
        coil[1, rows] = sre * pim + sim * pre
    for load in loads[:4]:
        load.wait()
    for slot in range(NSEG):
        for t in range(OT):
            w, at = weight(slot, t)
            blk[slot, t * BR : (t + 1) * BR] = (coil[0, at] * w).astype(BF16)
            blk[slot, KR + t * BR : KR + (t + 1) * BR] = (coil[1, at] * w).astype(BF16)
        got = mm(g[slot], blk[slot]).astype(BF16)
        first[slot * KR : (slot + 1) * KR, :NX] = got[:KR]
        first[slot * KR : (slot + 1) * KR, NX:] = got[KR:]
    for load in loads[4:]:
        load.wait()
    for pair in range(NSEG // 2):
        spec = mm(first[pair * 2 * KR : (pair + 1) * 2 * KR], gx[0])
        tre, tim = 0.0, 0.0
        for half in range(2):
            re, im = spec[half * KR : (half + 1) * KR, :NX], spec[half * KR : (half + 1) * KR, NX:]
            c, s = turn[pair * 2 + half, 0], turn[pair * 2 + half, 1]
            tre = tre + (re * c + im * s)
            tim = tim + (im * c - re * s)
        ks[0] = tre if pair == 0 else ks[0] + tre
        ks[1] = tim if pair == 0 else ks[1] + tim
    def demod(pair):
        re, im = ks[0], ks[1]
        for half in range(2):
            c, s = turn[pair * 2 + half, 0], turn[pair * 2 + half, 1]
            here = slice((pair * 2 + half) * KR, (pair * 2 + half + 1) * KR)
            first[here, :NX] = (re * c - im * s).astype(BF16)
            first[here, NX:] = (im * c + re * s).astype(BF16)

    def back_mm(pair):
        back = mm(first[pair * 2 * KR : (pair + 1) * 2 * KR], gx[1]).astype(BF16)
        for half in range(2):
            blk[pair * 2 + half, :KR] = back[half * KR : (half + 1) * KR, :NX]
            blk[pair * 2 + half, KR:] = back[half * KR : (half + 1) * KR, NX:]

    def gather(pair):
        for half in range(2):
            slot = pair * 2 + half
            places = [weight(slot, t) for t in range(OT)]
            rows = jnp.concatenate([ft[c, at] for c in range(2) for _, at in places], axis=0)
            band = mm(rows, blk[slot])
            for t, (w, at) in enumerate(places):
                acc[0, at] += band[t * BR : (t + 1) * BR] * w
                acc[1, at] += band[KR + t * BR : KR + (t + 1) * BR] * w

    pairs = NSEG // 2
    demod(0)
    for pair in range(pairs + 1):
        if pair < pairs:
            back_mm(pair)
        if pair + 1 < pairs:
            demod(pair + 1)
        if pair:
            gather(pair - 1)
    saves = []
    for chunk in range(4):
        rows = slice(chunk * 64, chunk * 64 + 64)
        sre = mine[0, rows].astype(F32)
        sim = mine[1, rows].astype(F32)
        are, aim = acc[0, rows], acc[1, rows]
        out_re = (sre * are + sim * aim).reshape(8, ROWS, NX)
        out_im = (sre * aim - sim * are).reshape(8, ROWS, NX)
        here = slice(chunk * 8, chunk * 8 + 8)
        out_ref[here] = jnp.concatenate([out_re, out_im], axis=1).astype(BF16)
        saves.append(pltpu.make_async_copy(out_ref.at[here], out.at[here], out_sem.at[chunk]))
        saves[-1].start()
    for save in saves:
        save.wait()


def applied_kernel(parts_ref, r_ref, p_ref, low_ref, high_ref, applied_ref, sums_ref):
    totals = [jnp.zeros((ROWS, NX), F32) for _ in range(4)]
    for q in range(2):
        total = jnp.zeros((2 * ROWS, NX), F32)
        for pair in range(2):
            for xc in range(8):
                total = total + parts_ref[(pair * 2 + q) * 8 + xc].astype(F32)
        for c in range(2):
            p = p_ref[0, q, c]
            r = r_ref[0, q, c]
            smooth = 2.0 * p - low_ref[0, q, c].astype(F32) - high_ref[0, q, c].astype(F32)
            applied = total[c * ROWS : (c + 1) * ROWS] + reg_weight * smooth + shift_weight * p
            applied_ref[0, q, c] = applied
            for i, term in enumerate((r * r, p * applied, r * applied, applied * applied)):
                totals[i] = totals[i] + term
    lane = lax.broadcasted_iota(jnp.int32, (8, 128), 1)
    line = jnp.zeros((8, 128), F32)
    for i in range(4):
        whole = jnp.sum(jnp.sum(totals[i], axis=0, keepdims=True), axis=1, keepdims=True)
        line = jnp.where(lane == i, whole, line)
    sums_ref[...] = jnp.broadcast_to(line[:1, :8], (DEVICES, 8))


def update_kernel(sums_ref, x_ref, r_ref, p_ref, applied_ref, x_out, r_out, p_out):
    sums = jnp.sum(sums_ref[...], axis=0, keepdims=True)
    rr, pa, ra, aa = (sums[:, i : i + 1] for i in range(4))
    alpha = rr / (pa + epsilon)
    rnew = rr - 2.0 * alpha * ra + alpha * alpha * aa
    beta = rnew / (rr + epsilon)
    alpha = jnp.broadcast_to(alpha, (ROWS, NX))
    beta = jnp.broadcast_to(beta, (ROWS, NX))
    for q in range(2):
        for c in range(2):
            p = p_ref[0, q, c]
            r = r_ref[0, q, c] - alpha * applied_ref[0, q, c]
            x_out[0, q, c] = x_ref[0, q, c] + alpha * p
            r_out[0, q, c] = r
            p_out[0, q, c] = r + beta * p


VM = pl.BlockSpec(memory_space=pltpu.VMEM)
HB = pl.BlockSpec(memory_space=pltpu.HBM)


def hbm(array):
    return pltpu.with_memory_space_constraint(array, pltpu.HBM)


def local(x_in, r_in, p_in, sens, seg_weights, seg_freq, band_ids, seg_count, k_bands):
    half_shape = jax.ShapeDtypeStruct((SEGS_DEV, HALF, BR, NX), BF16)
    send, same, other = pl.pallas_call(
        prep_kernel,
        in_specs=[HB, HB],
        out_specs=[HB, VM, VM],
        out_shape=[pltpu.HBM((GROUP, 2 * ROWS, NX), jnp.int16), half_shape, half_shape],
        scratch_shapes=[
            pltpu.VMEM((1, 2, 2, ROWS, NX), F32),
            pltpu.VMEM((SEGS_DEV, HALF, 2, BR, NX), BF16),
            pltpu.VMEM((2, 8, 2 * ROWS, NX), jnp.int16),
            pltpu.SemaphoreType.DMA((2,)),
            pltpu.SemaphoreType.DMA((4,)),
        ],
        compiler_params=pltpu.CompilerParams(vmem_limit_bytes=4 << 20),
        name="prep",
    )(hbm(p_in), hbm(seg_weights))
    halves = [
        lax.ppermute(same if k == 2 else other, "segments", [(i, (i + k) % 4) for i in range(4)])
        for k in (1, 2, 3)
    ]
    whole = lax.all_to_all(send, SPACE, 0, 0, tiled=True)
    halo = p_in.astype(BF16)
    low = lax.ppermute(halo, "frames", [(i, (i + 1) % 8) for i in range(8)])
    high = lax.ppermute(halo, "frames", [(i, (i + 7) % 8) for i in range(8)])
    bands = hbm(band_ids.T)
    g, ft, gx, elapsed, quarter, mine = pl.pallas_call(
        tables_kernel,
        in_specs=[HB] * 4,
        out_specs=[VM] * 6,
        out_shape=[
            jax.ShapeDtypeStruct((NSEG, 2 * KR, 2 * KR), BF16),
            jax.ShapeDtypeStruct((2, NY, 2 * KR), BF16),
            jax.ShapeDtypeStruct((2, NX, NX), BF16),
            jax.ShapeDtypeStruct((KR, NX), F32),
            jax.ShapeDtypeStruct((NSEG, 1, NX), F32),
            jax.ShapeDtypeStruct((2, NY, NX), BF16),
        ],
        scratch_shapes=[
            pltpu.VMEM((2, 2 * KR, NY), BF16),
            pltpu.SMEM((OT, NSEG), jnp.int32),
            pltpu.SMEM((1, KR // KB), jnp.int32),
            pltpu.SMEM((NSEG,), F32),
            pltpu.SemaphoreType.DMA((4,)),
        ],
        compiler_params=pltpu.CompilerParams(vmem_limit_bytes=32 << 20),
        cost_estimate=pl.CostEstimate(flops=1_000_000_000, bytes_accessed=2 << 20, transcendentals=0),
        name="tables",
    )(bands, hbm(k_bands), hbm(seg_freq), hbm(sens))
    turn = pl.pallas_call(
        turns_kernel,
        in_specs=[VM, VM] + [pl.BlockSpec(memory_space=pl.ANY)] * 3,
        out_specs=HB,
        out_shape=pltpu.HBM((NSEG, 2, KR, NX), F32),
        scratch_shapes=[pltpu.VMEM((NSEG, 2, KR, NX), F32), pltpu.SemaphoreType.DMA((NSEG,))],
        compiler_params=pltpu.CompilerParams(vmem_limit_bytes=32 << 20),
        cost_estimate=pl.CostEstimate(flops=40_000_000_000, bytes_accessed=3 << 20, transcendentals=0),
        name="turns",
    )(elapsed, quarter, *halves)
    others = [lax.ppermute(half, "coils", [(i, i ^ 1) for i in range(8)]) for half in halves]
    parts = pl.pallas_call(
        normal_kernel,
        in_specs=[HB] * 2 + [VM] * 11 + [HB] * 2,
        out_specs=HB,
        out_shape=pltpu.HBM((GROUP, 2 * ROWS, NX), BF16),
        scratch_shapes=[
            pltpu.VMEM((2, NY, NX), F32),
            pltpu.VMEM((NSEG, 2 * KR, NX), BF16),
            pltpu.VMEM((NSEG * KR, 2 * NX), BF16),
            pltpu.VMEM((2, KR, NX), F32),
            pltpu.VMEM((2, NY, NX), F32),
            pltpu.VMEM((2, SEGS_DEV, HALF, BR, NX), BF16),
            pltpu.VMEM((2, 2 * NX, 2 * NX), BF16),
            pltpu.VMEM((NSEG, 2, KR, NX), F32),
            pltpu.VMEM((GROUP, 2 * ROWS, NX), BF16),
            pltpu.SMEM((OT, NSEG), jnp.int32),
            pltpu.SMEM((NSEG,), jnp.int32),
            pltpu.SemaphoreType.DMA((10,)),
            pltpu.SemaphoreType.DMA((4,)),
        ],
        compiler_params=pltpu.CompilerParams(vmem_limit_bytes=32 << 20),
        cost_estimate=pl.CostEstimate(flops=2_400_000_000, bytes_accessed=8 << 20, transcendentals=0),
        name="normal",
    )(
        bands, hbm(seg_count), whole, g, ft, gx,
        halves[0], others[0], halves[1], others[1], halves[2], others[2], mine, hbm(seg_weights), hbm(turn),
    )
    parts = lax.all_to_all(parts, SPACE, 0, 0, tiled=True)
    share = jax.ShapeDtypeStruct(p_in.shape, F32)
    applied, sums = pl.pallas_call(
        applied_kernel,
        in_specs=[VM] * 5,
        out_specs=[VM, VM],
        out_shape=[share, jax.ShapeDtypeStruct((DEVICES, 8), F32)],
        compiler_params=pltpu.CompilerParams(vmem_limit_bytes=4 << 20),
        name="applied",
    )(parts, r_in, p_in, low, high)
    sums = lax.all_to_all(sums, ("frames", "segments", "coils"), 0, 0, tiled=True)
    return tuple(
        pl.pallas_call(
            update_kernel,
            in_specs=[VM] * 5,
            out_specs=[VM] * 3,
            out_shape=[share] * 3,
            compiler_params=pltpu.CompilerParams(vmem_limit_bytes=4 << 20),
            name="update",
        )(sums, x_in, r_in, p_in, applied)
    )


def solution(mesh):
    image = P("frames", None, None, ("segments", "coils"), None)
    in_specs = (
        image,
        image,
        image,
        P("coils", None, None, None, None),
        P("segments", None, None, None, None),
        P(),
        P(),
        P(),
        P("frames", None),
    )
    return jax.shard_map(local, mesh=mesh, in_specs=in_specs, out_specs=(image,) * 3, check_vma=False)
```

```python
import math

import jax
import jax.numpy as jnp
from jax import lax
from jax.experimental import pallas as pl
from jax.experimental.pallas import tpu as pltpu
from jax.sharding import PartitionSpec as P

BR = 16
KB = 8
NX = 256
NY = 256
OT = 8
NSEG = 12
KR = 128
SEGS_DEV = 3
YDEV = 4
GROUP = 32
ROWS = 8
HALF = OT // 2
DEVICES = 256
CODE = 32767.0 / 6.0

reg_weight = 0.5
shift_weight = 0.1
epsilon = 1e-06

F32 = jnp.float32
BF16 = jnp.bfloat16
SPACE = ("segments", "coils")


def sin_cos(quarter):
    sq = quarter * quarter
    s = F32(1.0 / math.factorial(9))
    for n in (7, 5, 3, 1):
        s = s * sq + F32((-1.0) ** (n // 2) / math.factorial(n))
    s = s * quarter
    c = F32(-1.0 / math.factorial(10))
    for n in (8, 6, 4, 2, 0):
        c = c * sq + F32((-1.0) ** (n // 2) / math.factorial(n))
    twice = s + s
    s, c = twice * c, 1.0 - twice * s
    twice = s + s
    return twice * c, 1.0 - twice * s


def unit_parts(products):
    n = ((products + 128) & 255) - 128
    s, c = sin_cos(n.astype(F32) * F32(0.5 * math.pi / 256))
    return c * F32(1.0 / 16.0), s * F32(-1.0 / 16.0)


def segment_of(slot):
    y = lax.axis_index("segments")
    return lax.rem(y - slot // SEGS_DEV + YDEV, YDEV) * SEGS_DEV + slot % SEGS_DEV


def block_of(place):
    core = lax.rem(lax.axis_index("coils"), 2)
    return lax.rem(core * HALF + place, OT)


def spread(values, index, width):
    out = jnp.zeros_like(index)
    for j, value in enumerate(values):
        out = jnp.where(index // width == j, value * width + index % width, out)
    return out


def prep_kernel(p_in, w_in, send_out, same_ref, other_ref, p_ref, w_ref, code, sem, send_sem):
    plane = lax.rem(lax.axis_index("segments"), 2)
    core = lax.rem(lax.axis_index("coils"), 2)
    load_p = pltpu.make_async_copy(p_in, p_ref, sem.at[0])
    load_w = pltpu.make_async_copy(w_in.at[:, pl.ds(core * HALF, HALF)], w_ref, sem.at[1])
    load_p.start()
    load_w.start()
    load_p.wait()
    saves = []
    for q in range(2):
        both = jnp.concatenate([p_ref[0, q, 0], p_ref[0, q, 1]], axis=0)
        value = jnp.floor(both * F32(CODE) + 0.5).astype(jnp.int32).astype(jnp.int16)
        for xc in range(8):
            code[q, xc] = value
        for pair in range(2):
            target = send_out.at[pl.ds((pair * 2 + q) * 8, 8)]
            saves.append(pltpu.make_async_copy(code.at[q], target, send_sem.at[pair * 2 + q]))
            saves[-1].start()
    load_w.wait()
    for i in range(SEGS_DEV):
        for t in range(HALF):
            same_ref[i, t] = w_ref[i, t, plane]
            other_ref[i, t] = w_ref[i, t, 1 - plane]
    for save in saves:
        save.wait()


def turns_kernel(elapsed_ref, freq_ref, h1, h2, h3, turn_out, turn, turn_sem):
    saves = [pltpu.make_async_copy(turn.at[slot], turn_out.at[slot], turn_sem.at[slot]) for slot in range(NSEG)]
    for slot in range(NSEG):
        turn[slot, 1], turn[slot, 0] = sin_cos(freq_ref[slot] * elapsed_ref[...])
        saves[slot].start()
    for save in saves:
        save.wait()


def tables_kernel(
    bands_in, kb_in, freq_in, sens_in, g_ref, ft, gx_ref, elapsed_ref, quarter_ref, mine_ref, e, bands_ref, kb_ref, freq_ref, sem
):
    loads = [
        pltpu.make_async_copy(source, target, sem.at[i])
        for i, (source, target) in enumerate([(bands_in, bands_ref), (kb_in, kb_ref), (freq_in, freq_ref)])
    ]
    y = lax.axis_index("segments")
    fetch = pltpu.make_async_copy(sens_in.at[y // 2, lax.rem(y, 2)], mine_ref, sem.at[3])
    for load in loads:
        load.start()
    fetch.start()
    rows = lax.broadcasted_iota(jnp.int32, (NX, NX), 0)
    cols = lax.broadcasted_iota(jnp.int32, (NX, NX), 1)
    re, im = unit_parts(rows * cols)
    gx_ref[0] = re.astype(BF16)
    gx_ref[1] = im.astype(BF16)
    for load in loads:
        load.wait()
    for slot in range(NSEG):
        quarter_ref[slot] = jnp.broadcast_to(freq_ref[segment_of(slot)] * F32(0.25), (1, NX))
    kbs = [kb_ref[0, j] for j in range(KR // KB)]
    ky_col = spread(kbs, lax.broadcasted_iota(jnp.int32, (KR, KR), 0), KB)
    ky_wide = jnp.concatenate([ky_col, ky_col], axis=1)
    cy = (((ky_wide + 128) & 255) - 128).astype(F32) * F32(1.0 / 128.0)
    cx_index = lax.broadcasted_iota(jnp.int32, (KR, NX), 1)
    cx = (((cx_index + 128) & 255) - 128).astype(F32) * F32(1.0 / 128.0)
    elapsed_ref[...] = jnp.sqrt(cy * cy + cx * cx)
    ky_row = spread(kbs, lax.broadcasted_iota(jnp.int32, (8, KR), 1), KB)[:1]
    re, im = unit_parts(lax.broadcasted_iota(jnp.int32, (NY, KR), 0) * ky_row)
    ft[0, :, :KR] = re.astype(BF16)
    ft[0, :, KR:] = im.astype(BF16)
    ft[1, :, :KR] = (-im).astype(BF16)
    ft[1, :, KR:] = re.astype(BF16)
    re, im = unit_parts(ky_wide * lax.broadcasted_iota(jnp.int32, (KR, NY), 1))
    e[0, :KR] = re.astype(BF16)
    e[0, KR:] = im.astype(BF16)
    e[1, :KR] = (-im).astype(BF16)
    e[1, KR:] = re.astype(BF16)
    image_row = lax.broadcasted_iota(jnp.int32, (NY, KR), 0)
    for slot in range(NSEG):
        seg = segment_of(slot)
        bands = [bands_ref[block_of(t), seg] for t in range(OT)]
        yr_row = spread(bands, lax.broadcasted_iota(jnp.int32, (8, KR), 1), BR)[:1]
        pick = jnp.where(image_row == yr_row, F32(1), F32(0)).astype(BF16)
        g_ref[slot, :, :KR] = mm(e[0], pick).astype(BF16)
        g_ref[slot, :, KR:] = mm(e[1], pick).astype(BF16)
    fetch.wait()


def mm(a, b):
    return jnp.dot(a, b, preferred_element_type=F32)


def normal_kernel(
    bands_in, count_in, low_any, p_ref, g, ft, gx_ref, h1, o1, h2, o2, h3, o3, mine, w_in, turn_in, out,
    coil, blk, first, ks, acc, near, gx, turn, out_ref, bands_ref, count_ref, sem, out_sem,
):
    y = lax.axis_index("segments")
    plane = lax.rem(y, 2)
    core = lax.rem(lax.axis_index("coils"), 2)
    loads = [
        pltpu.make_async_copy(source, target, sem.at[i])
        for i, (source, target) in enumerate(
            [
                (w_in.at[:, pl.ds(core * HALF, HALF), plane], near.at[0]),
                (w_in.at[:, pl.ds((1 - core) * HALF, HALF), plane], near.at[1]),
                (bands_in, bands_ref),
                (count_in, count_ref),
                *((turn_in.at[i : i + 2], turn.at[i : i + 2]) for i in range(0, NSEG, 2)),
            ]
        )
    ]
    for load in loads:
        load.start()
    halves = ((near.at[0], near.at[1]), (h1, o1), (h2, o2), (h3, o3))
    gre, gim = gx_ref[0], gx_ref[1]
    for i, sign in enumerate((1, -1)):
        gx[i, :NX, :NX] = gre
        gx[i, :NX, NX:] = sign * gim
        gx[i, NX:, :NX] = -sign * gim
        gx[i, NX:, NX:] = gre

    def weight(slot, t):
        seg = segment_of(slot)
        j = block_of(t)
        live = (j < count_ref[seg]).astype(F32)
        w = halves[slot // SEGS_DEV][t // HALF][slot % SEGS_DEV, t % HALF]
        at = pl.ds(pl.multiple_of(bands_ref[j, seg] * BR, BR), BR)
        return w.astype(F32) * live, at

    acc[...] = jnp.zeros_like(acc)
    for chunk in range(4):
        rows = slice(chunk * 64, chunk * 64 + 64)
        p = p_ref[chunk * 8 : chunk * 8 + 8].astype(jnp.int32).astype(F32) * F32(1.0 / CODE)
        pre = p[:, :ROWS].reshape(64, NX)
        pim = p[:, ROWS:].reshape(64, NX)
        sre = mine[0, rows].astype(F32)
        sim = mine[1, rows].astype(F32)
        coil[0, rows] = sre * pre - sim * pim
        coil[1, rows] = sre * pim + sim * pre
    for load in loads[:4]:
        load.wait()
    for slot in range(NSEG):
        for t in range(OT):
            w, at = weight(slot, t)
            blk[slot, t * BR : (t + 1) * BR] = (coil[0, at] * w).astype(BF16)
            blk[slot, KR + t * BR : KR + (t + 1) * BR] = (coil[1, at] * w).astype(BF16)
        got = mm(g[slot], blk[slot]).astype(BF16)
        first[slot * KR : (slot + 1) * KR, :NX] = got[:KR]
        first[slot * KR : (slot + 1) * KR, NX:] = got[KR:]
    for load in loads[4:]:
        load.wait()
    for pair in range(NSEG // 2):
        spec = mm(first[pair * 2 * KR : (pair + 1) * 2 * KR], gx[0])
        tre, tim = 0.0, 0.0
        for half in range(2):
            re, im = spec[half * KR : (half + 1) * KR, :NX], spec[half * KR : (half + 1) * KR, NX:]
            c, s = turn[pair * 2 + half, 0], turn[pair * 2 + half, 1]
            tre = tre + (re * c + im * s)
            tim = tim + (im * c - re * s)
        ks[0] = tre if pair == 0 else ks[0] + tre
        ks[1] = tim if pair == 0 else ks[1] + tim
    def demod(pair):
        re, im = ks[0], ks[1]
        for half in range(2):
            c, s = turn[pair * 2 + half, 0], turn[pair * 2 + half, 1]
            here = slice((pair * 2 + half) * KR, (pair * 2 + half + 1) * KR)
            first[here, :NX] = (re * c - im * s).astype(BF16)
            first[here, NX:] = (im * c + re * s).astype(BF16)

    def back_mm(pair):
        back = mm(first[pair * 2 * KR : (pair + 1) * 2 * KR], gx[1]).astype(BF16)
        for half in range(2):
            blk[pair * 2 + half, :KR] = back[half * KR : (half + 1) * KR, :NX]
            blk[pair * 2 + half, KR:] = back[half * KR : (half + 1) * KR, NX:]

    def gather(pair):
        for half in range(2):
            slot = pair * 2 + half
            places = [weight(slot, t) for t in range(OT)]
            rows = jnp.concatenate([ft[c, at] for c in range(2) for _, at in places], axis=0)
            band = mm(rows, blk[slot])
            for t, (w, at) in enumerate(places):
                acc[0, at] += band[t * BR : (t + 1) * BR] * w
                acc[1, at] += band[KR + t * BR : KR + (t + 1) * BR] * w

    pairs = NSEG // 2
    demod(0)
    for pair in range(pairs + 1):
        if pair < pairs:
            back_mm(pair)
        if pair + 1 < pairs:
            demod(pair + 1)
        if pair:
            gather(pair - 1)
    saves = []
    for chunk in range(4):
        rows = slice(chunk * 64, chunk * 64 + 64)
        sre = mine[0, rows].astype(F32)
        sim = mine[1, rows].astype(F32)
        are, aim = acc[0, rows], acc[1, rows]
        out_re = (sre * are + sim * aim).reshape(8, ROWS, NX)
        out_im = (sre * aim - sim * are).reshape(8, ROWS, NX)
        here = slice(chunk * 8, chunk * 8 + 8)
        out_ref[here] = jnp.concatenate([out_re, out_im], axis=1).astype(BF16)
        saves.append(pltpu.make_async_copy(out_ref.at[here], out.at[here], out_sem.at[chunk]))
        saves[-1].start()
    for save in saves:
        save.wait()


def applied_kernel(parts_ref, r_ref, p_ref, low_ref, high_ref, applied_ref, sums_ref):
    totals = [jnp.zeros((ROWS, NX), F32) for _ in range(4)]
    for q in range(2):
        total = jnp.zeros((2 * ROWS, NX), F32)
        for pair in range(2):
            for xc in range(8):
                total = total + parts_ref[(pair * 2 + q) * 8 + xc].astype(F32)
        for c in range(2):
            p = p_ref[0, q, c]
            r = r_ref[0, q, c]
            smooth = 2.0 * p - low_ref[0, q, c].astype(F32) - high_ref[0, q, c].astype(F32)
            applied = total[c * ROWS : (c + 1) * ROWS] + reg_weight * smooth + shift_weight * p
            applied_ref[0, q, c] = applied
            for i, term in enumerate((r * r, p * applied, r * applied, applied * applied)):
                totals[i] = totals[i] + term
    lane = lax.broadcasted_iota(jnp.int32, (8, 128), 1)
    line = jnp.zeros((8, 128), F32)
    for i in range(4):
        whole = jnp.sum(jnp.sum(totals[i], axis=0, keepdims=True), axis=1, keepdims=True)
        line = jnp.where(lane == i, whole, line)
    sums_ref[...] = jnp.broadcast_to(line[:1, :8], (DEVICES, 8))


def update_kernel(sums_ref, x_ref, r_ref, p_ref, applied_ref, x_out, r_out, p_out):
    sums = jnp.sum(sums_ref[...], axis=0, keepdims=True)
    rr, pa, ra, aa = (sums[:, i : i + 1] for i in range(4))
    alpha = rr / (pa + epsilon)
    rnew = rr - 2.0 * alpha * ra + alpha * alpha * aa
    beta = rnew / (rr + epsilon)
    alpha = jnp.broadcast_to(alpha, (ROWS, NX))
    beta = jnp.broadcast_to(beta, (ROWS, NX))
    for q in range(2):
        for c in range(2):
            p = p_ref[0, q, c]
            r = r_ref[0, q, c] - alpha * applied_ref[0, q, c]
            x_out[0, q, c] = x_ref[0, q, c] + alpha * p
            r_out[0, q, c] = r
            p_out[0, q, c] = r + beta * p


VM = pl.BlockSpec(memory_space=pltpu.VMEM)
HB = pl.BlockSpec(memory_space=pltpu.HBM)


def hbm(array):
    return pltpu.with_memory_space_constraint(array, pltpu.HBM)


def local(x_in, r_in, p_in, sens, seg_weights, seg_freq, band_ids, seg_count, k_bands):
    half_shape = jax.ShapeDtypeStruct((SEGS_DEV, HALF, BR, NX), BF16)
    send, same, other = pl.pallas_call(
        prep_kernel,
        in_specs=[HB, HB],
        out_specs=[HB, VM, VM],
        out_shape=[pltpu.HBM((GROUP, 2 * ROWS, NX), jnp.int16), half_shape, half_shape],
        scratch_shapes=[
            pltpu.VMEM((1, 2, 2, ROWS, NX), F32),
            pltpu.VMEM((SEGS_DEV, HALF, 2, BR, NX), BF16),
            pltpu.VMEM((2, 8, 2 * ROWS, NX), jnp.int16),
            pltpu.SemaphoreType.DMA((2,)),
            pltpu.SemaphoreType.DMA((4,)),
        ],
        compiler_params=pltpu.CompilerParams(vmem_limit_bytes=4 << 20),
        name="prep",
    )(hbm(p_in), hbm(seg_weights))
    halves = [
        lax.ppermute(same if k == 2 else other, "segments", [(i, (i + k) % 4) for i in range(4)])
        for k in (1, 2, 3)
    ]
    whole = lax.all_to_all(send, SPACE, 0, 0, tiled=True)
    halo = p_in.astype(BF16)
    low = lax.ppermute(halo, "frames", [(i, (i + 1) % 8) for i in range(8)])
    high = lax.ppermute(halo, "frames", [(i, (i + 7) % 8) for i in range(8)])
    bands = hbm(band_ids.T)
    g, ft, gx, elapsed, quarter, mine = pl.pallas_call(
        tables_kernel,
        in_specs=[HB] * 4,
        out_specs=[VM] * 6,
        out_shape=[
            jax.ShapeDtypeStruct((NSEG, 2 * KR, 2 * KR), BF16),
            jax.ShapeDtypeStruct((2, NY, 2 * KR), BF16),
            jax.ShapeDtypeStruct((2, NX, NX), BF16),
            jax.ShapeDtypeStruct((KR, NX), F32),
            jax.ShapeDtypeStruct((NSEG, 1, NX), F32),
            jax.ShapeDtypeStruct((2, NY, NX), BF16),
        ],
        scratch_shapes=[
            pltpu.VMEM((2, 2 * KR, NY), BF16),
            pltpu.SMEM((OT, NSEG), jnp.int32),
            pltpu.SMEM((1, KR // KB), jnp.int32),
            pltpu.SMEM((NSEG,), F32),
            pltpu.SemaphoreType.DMA((4,)),
        ],
        compiler_params=pltpu.CompilerParams(vmem_limit_bytes=32 << 20),
        cost_estimate=pl.CostEstimate(flops=1_000_000_000, bytes_accessed=2 << 20, transcendentals=0),
        name="tables",
    )(bands, hbm(k_bands), hbm(seg_freq), hbm(sens))
    turn = pl.pallas_call(
        turns_kernel,
        in_specs=[VM, VM] + [pl.BlockSpec(memory_space=pl.ANY)] * 3,
        out_specs=HB,
        out_shape=pltpu.HBM((NSEG, 2, KR, NX), F32),
        scratch_shapes=[pltpu.VMEM((NSEG, 2, KR, NX), F32), pltpu.SemaphoreType.DMA((NSEG,))],
        compiler_params=pltpu.CompilerParams(vmem_limit_bytes=32 << 20),
        cost_estimate=pl.CostEstimate(flops=40_000_000_000, bytes_accessed=3 << 20, transcendentals=0),
        name="turns",
    )(elapsed, quarter, *halves)
    others = [lax.ppermute(half, "coils", [(i, i ^ 1) for i in range(8)]) for half in halves]
    parts = pl.pallas_call(
        normal_kernel,
        in_specs=[HB] * 2 + [pl.BlockSpec(memory_space=pl.ANY)] + [VM] * 11 + [HB] * 2,
        out_specs=HB,
        out_shape=pltpu.HBM((GROUP, 2 * ROWS, NX), BF16),
        scratch_shapes=[
            pltpu.VMEM((2, NY, NX), F32),
            pltpu.VMEM((NSEG, 2 * KR, NX), BF16),
            pltpu.VMEM((NSEG * KR, 2 * NX), BF16),
            pltpu.VMEM((2, KR, NX), F32),
            pltpu.VMEM((2, NY, NX), F32),
            pltpu.VMEM((2, SEGS_DEV, HALF, BR, NX), BF16),
            pltpu.VMEM((2, 2 * NX, 2 * NX), BF16),
            pltpu.VMEM((NSEG, 2, KR, NX), F32),
            pltpu.VMEM((GROUP, 2 * ROWS, NX), BF16),
            pltpu.SMEM((OT, NSEG), jnp.int32),
            pltpu.SMEM((NSEG,), jnp.int32),
            pltpu.SemaphoreType.DMA((10,)),
            pltpu.SemaphoreType.DMA((4,)),
        ],
        compiler_params=pltpu.CompilerParams(vmem_limit_bytes=32 << 20),
        cost_estimate=pl.CostEstimate(flops=2_400_000_000, bytes_accessed=8 << 20, transcendentals=0),
        name="normal",
    )(
        bands, hbm(seg_count), low, whole, g, ft, gx,
        halves[0], others[0], halves[1], others[1], halves[2], others[2], mine, hbm(seg_weights), hbm(turn),
    )
    parts = lax.all_to_all(parts, SPACE, 0, 0, tiled=True)
    share = jax.ShapeDtypeStruct(p_in.shape, F32)
    applied, sums = pl.pallas_call(
        applied_kernel,
        in_specs=[VM] * 5,
        out_specs=[VM, VM],
        out_shape=[share, jax.ShapeDtypeStruct((DEVICES, 8), F32)],
        compiler_params=pltpu.CompilerParams(vmem_limit_bytes=4 << 20),
        name="applied",
    )(parts, r_in, p_in, low, high)
    sums = lax.all_to_all(sums, ("frames", "segments", "coils"), 0, 0, tiled=True)
    return tuple(
        pl.pallas_call(
            update_kernel,
            in_specs=[VM] * 5,
            out_specs=[VM] * 3,
            out_shape=[share] * 3,
            compiler_params=pltpu.CompilerParams(vmem_limit_bytes=4 << 20),
            name="update",
        )(sums, x_in, r_in, p_in, applied)
    )


def solution(mesh):
    image = P("frames", None, None, ("segments", "coils"), None)
    in_specs = (
        image,
        image,
        image,
        P("coils", None, None, None, None),
        P("segments", None, None, None, None),
        P(),
        P(),
        P(),
        P("frames", None),
    )
    return jax.shard_map(local, mesh=mesh, in_specs=in_specs, out_specs=(image,) * 3, check_vma=False)
```
